256 devices in a mesh: row: 32 (over z, y), col: 8 (over x, core).
Axes of the slice: x: 4, y: 4, z: 8, core: 2. Of those that a mesh axis runs over, the one named last changes fastest.
Arguments:
- factor: bfloat16 [28672, 28672], P('row', 'col'), as said below
- basis: bfloat16 [28672, 512], P('row'), may hold values from -6 to 6
Outputs:
- eigen_basis: float32 [28672, 512], P(('row', 'col'))
- middle_basis: bfloat16 [28672, 512], P('col')
The draws below stay inside these ranges and needn't reach their ends.
Inputs may be any that keep to these rules, and one draw needn't show every extreme that they name: factor is exactly symmetric.
All inputs are finite; a program needn't handle non-finite values.
Results may differ from the reference program's by a relative error of at most 0.0029.
Values may be sent and summed in bfloat16 or wider, within the bound.
No kernel may reach another device: no remote copies, remote signals or barrier semaphores. Data moves between devices by JAX's collectives and lax.ppermute only.
A program may use at most 128 MiB of HBM per device.

```python
import math
import jax
import jax.numpy as jnp
from jax import lax

M = 28672
K = 512


def draw_factor(key, part):
    key = jax.random.fold_in(key, 11)
    first_key, second_key = jax.random.split(key, 2)
    raw = jax.random.normal(first_key, (M, M), jnp.float32)
    symmetric = (raw + raw.T) * (1.6 / math.sqrt(2.0 * M))
    index_float = jnp.arange(M, dtype=jnp.float32)
    ramp = 1.0 + 2.0 * index_float / (M - 1)
    centre = 307.0 * M / 512.0
    width = M / 1024.0
    bump = 1.0 + 5.0 * jnp.exp(-((index_float - centre) / width) ** 2)
    spread = jnp.exp(jax.random.uniform(second_key, (M,), jnp.float32, 0.0, math.log(2.0)))
    values = 3.5 * spread * ramp * bump
    index = jnp.arange(M)
    whole = jnp.where(index[:, None] == index[None, :], values[:, None], 0.0) + symmetric
    return whole.astype(jnp.bfloat16)


def levels(rng, shape, shards, smallest, top_value):
    factor_of = 1.0
    for position, shards_of in shards:
        draws = jax.random.uniform(jax.random.fold_in(jax.random.fold_in(rng, 6), position), (shards_of,), jnp.float32, smallest / len(shards), top_value / len(shards))
        factor_of = factor_of * jnp.repeat(jnp.exp(draws), shape[position] // shards_of).reshape((-1,) + (1,) * (len(shape) - 1 - position))
    return factor_of


def normal_values(own_key, dims, deviation, reach, cuts=(), held_as=jnp.bfloat16):
    entries = jax.random.normal(own_key, dims, jnp.float32) * deviation
    if len(cuts) > 0:
        entries = levels(own_key, dims, cuts, -0.22, 0.18) * entries
    return jnp.clip(entries, min=-reach, max=reach).astype(held_as)


def setup_inputs(seed: int = 0) -> dict:
    seeds = jax.random.split(jax.random.key(seed), 3)
    return {
        "factor": draw_factor(jax.random.fold_in(seeds[2], 71), 0),
        "basis": normal_values(seeds[1], (M, K), 1.0, 6.0, ((0, 32),)),
    }


def product(factor, basis):
    blocks = factor.reshape(32, M // 32, M)
    out = lax.map(lambda blk: jnp.dot(blk.astype(jnp.float32), basis.astype(jnp.float32), preferred_element_type=jnp.float32), blocks)
    return out.reshape(M, K)

def orthonormal(values):
    gram = jnp.dot(values.T.astype(jnp.float32), values.astype(jnp.float32), precision=lax.Precision.HIGHEST, preferred_element_type=jnp.float32)
    lower = jnp.linalg.cholesky(gram)
    inverse = lax.linalg.triangular_solve(lower, jnp.eye(K, dtype=jnp.float32), left_side=True, lower=True)
    return jnp.dot(values.astype(jnp.float32), inverse.T.astype(jnp.float32), precision=lax.Precision.HIGHEST, preferred_element_type=jnp.float32)

def reference(factor, basis):
    first = product(factor, basis)
    middle = (orthonormal(first) * math.sqrt(M)).astype(jnp.bfloat16)
    second = product(factor, middle)
    return (orthonormal(second) * math.sqrt(M), middle)
```

```python
import math

import jax
import jax.numpy as jnp
from jax import lax
from jax.experimental import pallas as pl
from jax.experimental.pallas import tpu as pltpu
from jax.sharding import PartitionSpec as P

M = 28672
K = 512
B = 128
R = 8


def dot(a, b, ca, cb):
    return lax.dot_general(a, b, (((ca,), (cb,)), ((), ())), precision=lax.Precision.HIGHEST,
                           preferred_element_type=jnp.float32)


def leaf(block):
    n = B // R
    w = [block[R * i:R * i + R, :] for i in range(n)]
    lane = lax.broadcasted_iota(jnp.int32, (R, B), 1)
    sub = lax.broadcasted_iota(jnp.int32, (R, B), 0)
    done = []
    for p in range(n):
        at = R * p
        top = w[p]
        inside = (lane >= at) & (lane < at + R)
        columns = [jnp.broadcast_to(top[:, at + j:at + j + 1], (R, B)) for j in range(R)]
        entry = {(i, j): jnp.broadcast_to(columns[j][i:i + 1, :], (R, B)) for i in range(R) for j in range(i + 1)}
        rhs = jnp.where(inside, jnp.where(lane - at == sub, 1.0, 0.0), top)
        row = [jnp.broadcast_to(rhs[i:i + 1, :], (R, B)) for i in range(R)]
        ratio = {}
        over = []
        for k in range(R):
            over.append(1.0 / entry[k, k])
            for i in range(k + 1, R):
                ratio[i, k] = entry[i, k] * over[k]
            for i in range(k + 1, R):
                for j in range(k + 1, i + 1):
                    entry[i, j] = entry[i, j] - ratio[i, k] * entry[j, k]
            for i in range(k + 1, R):
                row[i] = row[i] - ratio[i, k] * row[k]
        back = [None] * R
        for k in reversed(range(R)):
            z = row[k] * over[k]
            for i in range(k + 1, R):
                z = z - ratio[i, k] * back[i]
            back[k] = z
        out = row[0] * lax.rsqrt(entry[0, 0])
        for k in range(1, R):
            out = jnp.where(sub == k, row[k] * lax.rsqrt(entry[k, k]), out)
        done.append(jnp.where(lane < at + R, out, 0.0))
        for i in range(p + 1, n):
            new = jnp.where(inside, 0.0, w[i])
            for j in range(R):
                new = new - jnp.broadcast_to(w[i][:, at + j:at + j + 1], (R, B)) * back[j]
            w[i] = new
    return jnp.concatenate(done, axis=0)


def chol_inverse(gram_ref, out_ref, work):
    n = K // B
    work[...] = gram_ref[...]
    for b in range(n):
        at = B * b
        low = leaf(work[at:at + B, at:at + B])
        work[at:at + B, at:at + B] = jnp.where(
            lax.broadcasted_iota(jnp.int32, (B, B), 0) == lax.broadcasted_iota(jnp.int32, (B, B), 1), 1.0, 0.0)
        top = dot(low, work[at:at + B, :], 1, 0)
        out_ref[at:at + B, :] = jnp.where(lax.broadcasted_iota(jnp.int32, (B, K), 1) < at + B, top, 0.0)
        for i in range(b + 1, n):
            to = B * i
            work[to:to + B, at:at + B] = jnp.zeros((B, B), jnp.float32)
            work[to:to + B, :] = work[to:to + B, :] - dot(top[:, to:to + B], top, 0, 0)


def inverse_factor(gram):
    return pl.pallas_call(
        chol_inverse,
        out_shape=jax.ShapeDtypeStruct((K, K), jnp.float32),
        in_specs=[pl.BlockSpec(memory_space=pltpu.VMEM)],
        out_specs=pl.BlockSpec(memory_space=pltpu.VMEM),
        scratch_shapes=[pltpu.VMEM((K, K), jnp.float32)],
        compiler_params=pltpu.CompilerParams(vmem_limit_bytes=32 * 1024 * 1024),
        cost_estimate=pl.CostEstimate(flops=2 * K ** 3, bytes_accessed=8 * K * K, transcendentals=0),
    )(gram)


def summed_share(values, axis):
    size = lax.axis_size(axis)
    pieces = values.reshape(size, values.shape[0] // size, values.shape[1])
    return jnp.sum(lax.all_to_all(pieces, axis, 0, 0, tiled=True), axis=0)


def column_rows(rows):
    height, width = lax.axis_size("row"), lax.axis_size("col")
    pairs = [(j, (j % height) * width + j // height) for j in range(height * width)]
    moved = lax.ppermute(rows, ("row", "col"), pairs)
    return lax.all_gather(moved, "row", axis=0, tiled=True)


def gram_inverse(values):
    gram = dot(values, values, 0, 0)
    share = summed_share(summed_share(gram, "col"), "row")
    whole = lax.all_gather(lax.all_gather(share, "row", axis=0, tiled=True), "col", axis=0, tiled=True)
    return inverse_factor(whole)


def shards(factor, basis):
    scale = math.sqrt(M)
    part = basis.shape[0] // lax.axis_size("col")
    own = lax.dynamic_slice_in_dim(basis, lax.axis_index("col") * part, part, 0)
    first = summed_share(jnp.dot(factor, column_rows(own), preferred_element_type=jnp.float32), "col")
    middle = (dot(first, gram_inverse(first), 1, 1) * scale).astype(jnp.bfloat16)
    column_basis = column_rows(middle)
    second = summed_share(jnp.dot(factor, column_basis, preferred_element_type=jnp.float32), "col")
    return (dot(second, gram_inverse(second), 1, 1) * scale, column_basis)


def solution(mesh):
    return jax.shard_map(
        shards,
        mesh=mesh,
        in_specs=(P("row", "col"), P("row", None)),
        out_specs=(P(("row", "col"), None), P("col", None)),
        check_vma=False,
    )
```

```python
import math

import jax
import jax.numpy as jnp
from jax import lax
from jax.experimental import pallas as pl
from jax.experimental.pallas import tpu as pltpu
from jax.sharding import PartitionSpec as P

M = 28672
K = 512
B = 128
R = 8
AXES = ("z", "y", "x", "core")
SIZES = (8, 4, 4, 2)
HALF = K // 2
ROWS = M // 256


def dot(a, b, ca, cb):
    return lax.dot_general(a, b, (((ca,), (cb,)), ((), ())), precision=lax.Precision.HIGHEST,
                           preferred_element_type=jnp.float32)


def leaf(block):
    n = B // R
    w = [block[R * i:R * i + R, :] for i in range(n)]
    lane = lax.broadcasted_iota(jnp.int32, (R, B), 1)
    sub = lax.broadcasted_iota(jnp.int32, (R, B), 0)
    done = []
    for p in range(n):
        at = R * p
        top = w[p]
        inside = (lane >= at) & (lane < at + R)
        columns = [jnp.broadcast_to(top[:, at + j:at + j + 1], (R, B)) for j in range(R)]
        entry = {(i, j): jnp.broadcast_to(columns[j][i:i + 1, :], (R, B)) for i in range(R) for j in range(i + 1)}
        rhs = jnp.where(inside, jnp.where(lane - at == sub, 1.0, 0.0), top)
        row = [jnp.broadcast_to(rhs[i:i + 1, :], (R, B)) for i in range(R)]
        ratio = {}
        over = []
        for k in range(R):
            over.append(1.0 / entry[k, k])
            for i in range(k + 1, R):
                ratio[i, k] = entry[i, k] * over[k]
            for i in range(k + 1, R):
                for j in range(k + 1, i + 1):
                    entry[i, j] = entry[i, j] - ratio[i, k] * entry[j, k]
            for i in range(k + 1, R):
                row[i] = row[i] - ratio[i, k] * row[k]
        back = [None] * R
        for k in reversed(range(R)):
            z = row[k] * over[k]
            for i in range(k + 1, R):
                z = z - ratio[i, k] * back[i]
            back[k] = z
        out = row[0] * lax.rsqrt(entry[0, 0])
        for k in range(1, R):
            out = jnp.where(sub == k, row[k] * lax.rsqrt(entry[k, k]), out)
        done.append(jnp.where(lane < at + R, out, 0.0))
        for i in range(p + 1, n):
            new = jnp.where(inside, 0.0, w[i])
            for j in range(R):
                new = new - jnp.broadcast_to(w[i][:, at + j:at + j + 1], (R, B)) * back[j]
            w[i] = new
    return jnp.concatenate(done, axis=0)


def chol_inverse(gram_ref, out_ref, work):
    n = K // B
    work[...] = gram_ref[...]
    for b in range(n):
        at = B * b
        low = leaf(work[at:at + B, at:at + B])
        work[at:at + B, at:at + B] = jnp.where(
            lax.broadcasted_iota(jnp.int32, (B, B), 0) == lax.broadcasted_iota(jnp.int32, (B, B), 1), 1.0, 0.0)
        top = dot(low, work[at:at + B, :], 1, 0)
        out_ref[at:at + B, :] = jnp.where(lax.broadcasted_iota(jnp.int32, (B, K), 1) < at + B, top, 0.0)
        for i in range(b + 1, n):
            to = B * i
            work[to:to + B, at:at + B] = jnp.zeros((B, B), jnp.float32)
            work[to:to + B, :] = work[to:to + B, :] - dot(top[:, to:to + B], top, 0, 0)


def inverse_factor(gram):
    return pl.pallas_call(
        chol_inverse,
        out_shape=jax.ShapeDtypeStruct((K, K), jnp.float32),
        in_specs=[pl.BlockSpec(memory_space=pltpu.VMEM)],
        out_specs=pl.BlockSpec(memory_space=pltpu.VMEM),
        scratch_shapes=[pltpu.VMEM((K, K), jnp.float32)],
        compiler_params=pltpu.CompilerParams(vmem_limit_bytes=32 * 1024 * 1024),
        cost_estimate=pl.CostEstimate(flops=2 * K ** 3, bytes_accessed=8 * K * K, transcendentals=0),
    )(gram)


def permute(values, where):
    places = [(z, y, x, c) for z in range(8) for y in range(4) for x in range(4) for c in range(2)]
    index = {place: i for i, place in enumerate(places)}
    return lax.ppermute(values, AXES, [(index[p], index[where(*p)]) for p in places])


def other_core(z, y, x, c):
    return z, y, x, 1 - c


def exchange(pieces, axes):
    return lax.all_to_all(pieces, axes, 0, 0, tiled=True)


def copies(values, axes):
    return jnp.broadcast_to(values[None], (lax.axis_size(axes),) + values.shape)


def rolled(pieces):
    rows = pieces[0].shape[0]
    twice = jnp.concatenate(pieces + pieces, axis=0)
    return lax.dynamic_slice_in_dim(twice, lax.rem(4 - lax.axis_index("y"), 4) * rows, 4 * rows, 0)


def gather_y(own):
    up = lambda z, y, x, c: (z, (y + 1) % 4, x, c)
    down = lambda z, y, x, c: (z, (y - 1) % 4, x, c)
    half = own.shape[0] // 2
    before, after = permute(own, up), permute(own, down)
    far = jnp.concatenate([permute(before[:half], up), permute(after[half:], down)], axis=0)
    return [own, after, far, before]


def spread(left, right):
    left, right = lax.optimization_barrier((left, right))
    return lax.all_gather(left, "z", axis=0, tiled=True), right


def basis_rows(basis):
    part = 4 * ROWS
    halves = basis.reshape(2, part, K)[:, :, :HALF]
    sent = lax.dynamic_slice_in_dim(halves, lax.axis_index("core"), 1, 0)[0]
    left = permute(sent, lambda z, y, x, c: (2 * y + c, x, z // 2, z % 2))
    right = permute(basis[:, HALF:], lambda z, y, x, c: (2 * x + c, y, z // 2, z % 2))
    left, right = spread(left, right)
    return left, gather_y(right)


def middle_rows(rows):
    def along_y(step):
        def where(z, y, x, c):
            chunk = 8 * y + 2 * x + c
            return chunk // 4, (chunk + step) % 4, z // 2, z % 2
        return where
    parts = [permute(rows[:, :HALF], along_y(step)) for step in range(4)]
    right = permute(rows[:, HALF:], lambda z, y, x, c: (2 * x + c, y, z // 2, z % 2))
    left = rolled([parts[0], parts[3], parts[2], parts[1]])
    left, right = spread(left, right)
    right = exchange(copies(right, "z"), "z").reshape(8 * ROWS, HALF)
    return left, gather_y(right)


def product_step(place, a_ref, left_ref, *refs):
    pieces, out_ref = refs[:4], refs[4]
    step = pl.program_id(0)
    a = a_ref[...].reshape(4 * ROWS, 8 * ROWS)
    left = left_ref[...]
    for j in range(4):
        @pl.when(step == j)
        def _():
            right = pieces[j][...]
            one = jnp.dot(a, left, preferred_element_type=jnp.float32).reshape(4, ROWS, HALF)
            two = jnp.dot(a, right, preferred_element_type=jnp.float32).reshape(4, ROWS, HALF)
            if j == 0:
                out_ref[:, :, :HALF] = one
                out_ref[:, :, HALF:] = two
            else:
                out_ref[:, :, :HALF] += one
                out_ref[:, :, HALF:] += two
            if len(refs) > 5:
                refs[5][:, :HALF] = left
                refs[5][:, HALF:] = right


def product(factor, left, pieces, core, keep):
    place = jnp.stack([lax.axis_index("y"), core]).astype(jnp.int32)
    block = lambda q, place: lax.rem(place[0] + q, 4)
    out_shape = [jax.ShapeDtypeStruct((4, ROWS, K), jnp.float32)]
    out_specs = [pl.BlockSpec((4, ROWS, K), lambda q, place: (0, 0, 0))]
    if keep:
        out_shape.append(jax.ShapeDtypeStruct((32 * ROWS, K), jnp.bfloat16))
        out_specs.append(pl.BlockSpec((8 * ROWS, K), lambda q, place: (block(q, place), 0)))
    return pl.pallas_call(
        product_step,
        out_shape=out_shape,
        grid_spec=pltpu.PrefetchScalarGridSpec(
            num_scalar_prefetch=1,
            grid=(4,),
            in_specs=[
                pl.BlockSpec((4, None, ROWS, 8 * ROWS), lambda q, place: (0, place[1], 0, block(q, place))),
                pl.BlockSpec((8 * ROWS, HALF), lambda q, place: (block(q, place), 0)),
            ] + [pl.BlockSpec((8 * ROWS, HALF), lambda q, place: (0, 0))] * 4,
            out_specs=out_specs,
        ),
        compiler_params=pltpu.CompilerParams(vmem_limit_bytes=40 * 1024 * 1024),
        cost_estimate=pl.CostEstimate(flops=2 * 4 * ROWS * 32 * ROWS * K, bytes_accessed=8 * 1024 * 1024, transcendentals=0),
    )(place, factor.reshape(4, 2, ROWS, 32 * ROWS), left, *pieces)


def summed_product(factor, left, pieces, keep):
    core = lax.axis_index("core")
    theirs = product(factor, left, pieces, 1 - core, False)[0]
    came = permute(theirs, other_core)
    mine = product(factor, left, pieces, core, keep)
    total = jnp.sum(exchange(mine[0] + came, "x"), axis=0)
    return total, mine[1] if keep else None


def gram_inverse(values):
    gram = dot(values, values, 0, 0)
    core = lax.axis_index("core")
    half = lambda which: lax.dynamic_slice_in_dim(gram, which * HALF, HALF, 0)
    share = half(core) + permute(half(1 - core), other_core)
    share = jnp.sum(exchange(share.reshape(16, HALF // 16, K), ("y", "x")), axis=0)
    share = jnp.sum(exchange(copies(share, "z"), "z"), axis=0)
    share = exchange(copies(share, ("y", "x")), ("y", "x")).reshape(HALF, K)
    came = permute(share, other_core)
    first = jnp.where(core == 0, share, came)
    second = jnp.where(core == 0, came, share)
    return inverse_factor(jnp.concatenate([first, second], axis=0))


def shards(factor, basis):
    scale = math.sqrt(M)
    left, pieces = basis_rows(basis)
    first, _ = summed_product(factor, left, pieces, False)
    middle = (dot(first, gram_inverse(first), 1, 1) * scale).astype(jnp.bfloat16)
    left, pieces = middle_rows(middle)
    second, column_basis = summed_product(factor, left, pieces, True)
    return dot(second, gram_inverse(second), 1, 1) * scale, column_basis


def solution(mesh):
    fine = jax.sharding.Mesh(mesh.devices.reshape(SIZES), AXES)
    return jax.shard_map(
        shards,
        mesh=fine,
        in_specs=(P(("z", "y"), ("x", "core")), P(("z", "y"), None)),
        out_specs=(P(AXES, None), P(("x", "core"), None)),
        check_vma=False,
    )
```

```python
import math

import jax
import jax.numpy as jnp
from jax import lax
from jax.experimental import pallas as pl
from jax.experimental.pallas import tpu as pltpu
from jax.sharding import PartitionSpec as P

M = 28672
K = 512
B = 128
R = 8
AXES = ("z", "y", "x", "core")
SIZES = (8, 4, 4, 2)
HALF = K // 2
FEW = 128
ROWS = M // 256


def dot(a, b, ca, cb):
    return lax.dot_general(a, b, (((ca,), (cb,)), ((), ())), precision=lax.Precision.HIGHEST,
                           preferred_element_type=jnp.float32)


def reciprocal_rows(top, at, lane, sub):
    wide = [jnp.broadcast_to(top[:, at + j:at + j + 1], (R, B)) for j in range(R)]
    e = {(i, j): jnp.broadcast_to(wide[j][i:i + 1, :], (R, B)) for i in range(R) for j in range(i + 1)}
    inside = (lane >= at) & (lane < at + R)
    rhs = jnp.where(inside, jnp.where(lane - at == sub, 1.0, 0.0), top)
    row = [jnp.broadcast_to(rhs[i:i + 1, :], (R, B)) for i in range(R)]
    ratio, solved, final = {}, [None] * R, [None] * R
    for k in range(0, R, 2):
        a, b, c = e[k, k], e[k + 1, k], e[k + 1, k + 1]
        det = a * c - b * b
        over = 1.0 / det
        for i in range(k + 2, R):
            ratio[i, k] = (e[i, k] * c - e[i, k + 1] * b) * over
            ratio[i, k + 1] = (e[i, k + 1] * a - e[i, k] * b) * over
        for i in range(k + 2, R):
            for j in range(k + 2, i + 1):
                e[i, j] = e[i, j] - (ratio[i, k] * e[j, k] + ratio[i, k + 1] * e[j, k + 1])
            row[i] = row[i] - (ratio[i, k] * row[k] + ratio[i, k + 1] * row[k + 1])
        solved[k] = (c * row[k] - b * row[k + 1]) * over
        solved[k + 1] = (a * row[k + 1] - b * row[k]) * over
        root = lax.rsqrt(a)
        final[k] = row[k] * root
        final[k + 1] = (row[k + 1] - (b * root) * final[k]) * (lax.rsqrt(det) * (a * root))
    back = [None] * R
    for k in reversed(range(R)):
        z = solved[k]
        for i in reversed(range(k + 2 - k % 2, R)):
            z = z - ratio[i, k] * back[i]
        back[k] = z
    out = final[0]
    for k in range(1, R):
        out = jnp.where(sub == k, final[k], out)
    return jnp.where(lane < at + R, out, 0.0), back, inside


def leaf(block):
    n = B // R
    w = [block[R * i:R * i + R, :] for i in range(n)]
    lane = lax.broadcasted_iota(jnp.int32, (R, B), 1)
    sub = lax.broadcasted_iota(jnp.int32, (R, B), 0)
    done = []
    for p in range(n):
        at = R * p
        rows, back, inside = reciprocal_rows(w[p], at, lane, sub)
        done.append(rows)
        for i in range(p + 1, n):
            new = jnp.where(inside, 0.0, w[i])
            for j in reversed(range(R)):
                new = new - jnp.broadcast_to(w[i][:, at + j:at + j + 1], (R, B)) * back[j]
            w[i] = new
    return jnp.concatenate(done, axis=0)


def unit(n):
    return lax.broadcasted_iota(jnp.int32, (n, n), 0) == lax.broadcasted_iota(jnp.int32, (n, n), 1)


def chol_inverse(gram_ref, out_ref, work):
    gram = gram_ref[...]
    diagonal = jnp.where(unit(K), gram, 0.0)
    along = lax.rsqrt(jnp.sum(diagonal, axis=0, keepdims=True))
    work[...] = gram * along * lax.rsqrt(jnp.sum(diagonal, axis=1, keepdims=True))

    def block(b, _):
        at = pl.multiple_of(b * B, B)
        low = leaf(work[pl.ds(at, B), pl.ds(at, B)])
        work[pl.ds(at, B), pl.ds(at, B)] = jnp.where(unit(B), 1.0, 0.0)
        top = dot(low, work[pl.ds(at, B), :], 1, 0)
        lane = lax.broadcasted_iota(jnp.int32, (B, K), 1)
        out_ref[pl.ds(at, B), :] = jnp.where(lane < at + B, top, 0.0) * along
        for i in range(1, K // B):
            @pl.when(i > b)
            def _():
                to = B * i
                work[to:to + B, pl.ds(at, B)] = jnp.zeros((B, B), jnp.float32)
                work[to:to + B, :] = work[to:to + B, :] - dot(top[:, to:to + B], top, 0, 0)
        return 0

    lax.fori_loop(0, K // B, block, 0)


def inverse_factor(gram):
    return pl.pallas_call(
        chol_inverse,
        out_shape=jax.ShapeDtypeStruct((K, K), jnp.float32),
        in_specs=[pl.BlockSpec(memory_space=pltpu.VMEM)],
        out_specs=pl.BlockSpec(memory_space=pltpu.VMEM),
        scratch_shapes=[pltpu.VMEM((K, K), jnp.float32)],
        compiler_params=pltpu.CompilerParams(vmem_limit_bytes=32 * 1024 * 1024),
        cost_estimate=pl.CostEstimate(flops=2 * K ** 3, bytes_accessed=8 * K * K, transcendentals=0),
    )(gram)


def permute(values, where):
    places = [(z, y, x, c) for z in range(8) for y in range(4) for x in range(4) for c in range(2)]
    index = {place: i for i, place in enumerate(places)}
    return lax.ppermute(values, AXES, [(index[p], index[where(*p)]) for p in places])


def other_core(z, y, x, c):
    return z, y, x, 1 - c


def exchange(pieces, axes):
    return lax.all_to_all(pieces, axes, 0, 0, tiled=True)


def copies(values, axes):
    return jnp.broadcast_to(values[None], (lax.axis_size(axes),) + values.shape)


def up(z, y, x, c):
    return z, (y + 1) % 4, x, c


def down(z, y, x, c):
    return z, (y - 1) % 4, x, c


def gather_y(own):
    half = own.shape[0] // 2
    before, after = permute(own, up), permute(own, down)
    far = jnp.concatenate([permute(before[:half], up), permute(after[half:], down)], axis=0)
    return [own, after, far, before]


def gather_y_small(own):
    far = permute(own, lambda z, y, x, c: (z, (y + 2) % 4, x, c))
    rows = own.shape[0]
    out = jnp.zeros((4 * rows, own.shape[1]), own.dtype)
    for step, piece in enumerate([own, permute(own, down), far, permute(own, up)]):
        out = lax.dynamic_update_slice_in_dim(out, piece, lax.rem(lax.axis_index("y") + step, 4) * rows, 0)
    return out


def column_block(z, y, x, c):
    return 2 * x + c, y, z // 2, z % 2


def spread(many, few):
    many, few = lax.optimization_barrier((many, few))
    return lax.all_gather(many, "z", axis=0, tiled=True), few


def basis_rows(basis):
    sent = lax.dynamic_slice(basis, (lax.axis_index("core") * 4 * ROWS, FEW), (4 * ROWS, K - FEW))
    many = permute(sent, lambda z, y, x, c: (2 * y + c, x, z // 2, z % 2))
    few = permute(basis[:, :FEW], column_block)
    many, few = spread(many, few)
    return many, gather_y(few)


def middle_rows(rows):
    def chunk_place(z, y, x, c):
        chunk = 8 * y + 2 * x + c
        return chunk // 4, chunk % 4, z // 2, z % 2
    many = permute(rows[:, FEW:], chunk_place)
    few = permute(rows[:, :FEW], column_block)
    many, few = spread(gather_y_small(many), few)
    return many, gather_y(exchange(copies(few, "z"), "z").reshape(8 * ROWS, FEW))


def few_step(place, a_ref, *refs):
    pieces, out_ref = refs[:4], refs[4]
    a = a_ref[...].reshape(4 * ROWS, 8 * ROWS)
    for j in range(4):
        @pl.when(pl.program_id(1) == j)
        def _():
            term = jnp.dot(a, pieces[j][...], preferred_element_type=jnp.float32).reshape(4, ROWS, FEW)
            if j == 0:
                out_ref[...] = term
            else:
                out_ref[...] += term


def product_few(factor, pieces):
    core = lax.axis_index("core")
    place = jnp.stack([lax.axis_index("y"), core]).astype(jnp.int32)
    return pl.pallas_call(
        few_step,
        out_shape=jax.ShapeDtypeStruct((2, 4, ROWS, FEW), jnp.float32),
        grid_spec=pltpu.PrefetchScalarGridSpec(
            num_scalar_prefetch=1,
            grid=(2, 4),
            in_specs=[
                pl.BlockSpec((4, None, ROWS, 8 * ROWS),
                             lambda h, q, place: (0, lax.rem(place[1] + 1 + h, 2), 0, lax.rem(place[0] + q, 4))),
            ] + [pl.BlockSpec((8 * ROWS, FEW), lambda h, q, place: (0, 0))] * 4,
            out_specs=pl.BlockSpec((None, 4, ROWS, FEW), lambda h, q, place: (h, 0, 0, 0)),
        ),
        compiler_params=pltpu.CompilerParams(vmem_limit_bytes=40 * 1024 * 1024),
        cost_estimate=pl.CostEstimate(flops=2 * 8 * ROWS * M // 8 * FEW, bytes_accessed=8 * 1024 * 1024, transcendentals=0),
    )(place, factor.reshape(4, 2, ROWS, 32 * ROWS), *pieces)


def many_step(place, a_ref, b_ref, *refs):
    step = pl.program_id(0)
    a = a_ref[...].reshape(4 * ROWS, 8 * ROWS)
    out_ref = refs[-1]
    if len(refs) > 1:
        pieces, out_ref, rows_ref = refs[:4], refs[4], refs[5]
        rows_ref[:, FEW:] = b_ref[...]
        for j in range(4):
            @pl.when(lax.rem(place[1] + j, 4) == step)
            def _():
                rows_ref[:, :FEW] = pieces[j][...]
    term = jnp.dot(a, b_ref[...], preferred_element_type=jnp.float32).reshape(out_ref.shape)

    @pl.when(step == 0)
    def _():
        out_ref[...] = term

    @pl.when(step > 0)
    def _():
        out_ref[...] += term


def product_many(factor, many, core, pieces=()):
    place = jnp.stack([core, lax.axis_index("y")]).astype(jnp.int32)
    out_shape = [jax.ShapeDtypeStruct((4, ROWS, K - FEW), jnp.float32)]
    out_specs = [pl.BlockSpec((4, ROWS, K - FEW), lambda q, place: (0, 0, 0))]
    if pieces:
        out_shape.append(jax.ShapeDtypeStruct((32 * ROWS, K), jnp.bfloat16))
        out_specs.append(pl.BlockSpec((8 * ROWS, K), lambda q, place: (q, 0)))
    return pl.pallas_call(
        many_step,
        out_shape=out_shape,
        grid_spec=pltpu.PrefetchScalarGridSpec(
            num_scalar_prefetch=1,
            grid=(4,),
            in_specs=[
                pl.BlockSpec((4, None, ROWS, 8 * ROWS), lambda q, place: (0, place[0], 0, q)),
                pl.BlockSpec((8 * ROWS, K - FEW), lambda q, place: (q, 0)),
            ] + [pl.BlockSpec((8 * ROWS, FEW), lambda q, place: (0, 0))] * len(pieces),
            out_specs=out_specs,
        ),
        compiler_params=pltpu.CompilerParams(vmem_limit_bytes=40 * 1024 * 1024),
        cost_estimate=pl.CostEstimate(flops=2 * 4 * ROWS * M // 8 * (K - FEW), bytes_accessed=8 * 1024 * 1024, transcendentals=0),
    )(place, factor.reshape(4, 2, ROWS, 32 * ROWS), many, *pieces)


def summed_product(factor, many, pieces, keep):
    core = lax.axis_index("core")
    both = product_few(factor, pieces)
    few = jnp.sum(exchange(both[1] + permute(both[0], other_core), "x"), axis=0)
    many, few = lax.optimization_barrier((many, few))
    came = permute(product_many(factor, many, 1 - core)[0], other_core)
    mine = product_many(factor, many, core, pieces if keep else [])
    total = jnp.sum(exchange(mine[0] + came, "x"), axis=0)
    return jnp.concatenate([few, total], axis=1), mine[-1]


def gram_inverse(values):
    gram = dot(values, values, 0, 0)
    core = lax.axis_index("core")
    half = lambda which: lax.dynamic_slice_in_dim(gram, which * HALF, HALF, 0)
    share = half(core) + permute(half(1 - core), other_core)
    share = jnp.sum(exchange(share.reshape(16, HALF // 16, K), ("y", "x")), axis=0)
    share = jnp.sum(exchange(copies(share, "z"), "z"), axis=0)
    share = exchange(copies(share, ("y", "x")), ("y", "x")).reshape(HALF, K)
    came = permute(share, other_core)
    first = jnp.where(core == 0, share, came)
    second = jnp.where(core == 0, came, share)
    return inverse_factor(jnp.concatenate([first, second], axis=0))


def shards(factor, basis):
    scale = math.sqrt(M)
    first, _ = summed_product(factor, *basis_rows(basis), False)
    middle = (dot(first, gram_inverse(first), 1, 1) * scale).astype(jnp.bfloat16)
    second, column_basis = summed_product(factor, *middle_rows(middle), True)
    return dot(second, gram_inverse(second), 1, 1) * scale, column_basis


def solution(mesh):
    fine = jax.sharding.Mesh(mesh.devices.reshape(SIZES), AXES)
    return jax.shard_map(
        shards,
        mesh=fine,
        in_specs=(P(("z", "y"), ("x", "core")), P(("z", "y"), None)),
        out_specs=(P(AXES, None), P(("x", "core"), None)),
        check_vma=False,
    )
```

```python
import math

import jax
import jax.numpy as jnp
from jax import lax
from jax.experimental import pallas as pl
from jax.experimental.pallas import tpu as pltpu
from jax.sharding import PartitionSpec as P

M = 28672
K = 512
B = 128
R = 8
AXES = ("z", "y", "x", "core")
SIZES = (8, 4, 4, 2)
HALF = K // 2
FEW_FIRST = 256
FEW_SECOND = 128
ROWS = M // 256


def dot(a, b, ca, cb):
    return lax.dot_general(a, b, (((ca,), (cb,)), ((), ())), precision=lax.Precision.HIGHEST,
                           preferred_element_type=jnp.float32)


def reciprocal_rows(top, at, lane, sub):
    wide = [jnp.broadcast_to(top[:, at + j:at + j + 1], (R, B)) for j in range(R)]
    e = {(i, j): jnp.broadcast_to(wide[j][i:i + 1, :], (R, B)) for i in range(R) for j in range(i + 1)}
    inside = (lane >= at) & (lane < at + R)
    rhs = jnp.where(inside, jnp.where(lane - at == sub, 1.0, 0.0), top)
    row = [jnp.broadcast_to(rhs[i:i + 1, :], (R, B)) for i in range(R)]
    ratio, solved, final = {}, [None] * R, [None] * R
    for k in range(0, R, 2):
        a, b, c = e[k, k], e[k + 1, k], e[k + 1, k + 1]
        det = a * c - b * b
        over = 1.0 / det
        for i in range(k + 2, R):
            ratio[i, k] = (e[i, k] * c - e[i, k + 1] * b) * over
            ratio[i, k + 1] = (e[i, k + 1] * a - e[i, k] * b) * over
        for i in range(k + 2, R):
            for j in range(k + 2, i + 1):
                e[i, j] = e[i, j] - (ratio[i, k] * e[j, k] + ratio[i, k + 1] * e[j, k + 1])
            row[i] = row[i] - (ratio[i, k] * row[k] + ratio[i, k + 1] * row[k + 1])
        solved[k] = (c * row[k] - b * row[k + 1]) * over
        solved[k + 1] = (a * row[k + 1] - b * row[k]) * over
        root = lax.rsqrt(a)
        final[k] = row[k] * root
        final[k + 1] = (row[k + 1] - (b * root) * final[k]) * (lax.rsqrt(det) * (a * root))
    back = [None] * R
    for k in reversed(range(R)):
        z = solved[k]
        for i in reversed(range(k + 2 - k % 2, R)):
            z = z - ratio[i, k] * back[i]
        back[k] = z
    out = final[0]
    for k in range(1, R):
        out = jnp.where(sub == k, final[k], out)
    return jnp.where(lane < at + R, out, 0.0), back, inside


def leaf(block):
    n = B // R
    w = [block[R * i:R * i + R, :] for i in range(n)]
    lane = lax.broadcasted_iota(jnp.int32, (R, B), 1)
    sub = lax.broadcasted_iota(jnp.int32, (R, B), 0)
    done = []
    for p in range(n):
        at = R * p
        rows, back, inside = reciprocal_rows(w[p], at, lane, sub)
        done.append(rows)
        for i in range(p + 1, n):
            new = jnp.where(inside, 0.0, w[i])
            for j in reversed(range(R)):
                new = new - jnp.broadcast_to(w[i][:, at + j:at + j + 1], (R, B)) * back[j]
            w[i] = new
    return jnp.concatenate(done, axis=0)


def unit(n):
    return lax.broadcasted_iota(jnp.int32, (n, n), 0) == lax.broadcasted_iota(jnp.int32, (n, n), 1)


def chol_inverse(gram_ref, out_ref, work):
    gram = gram_ref[...]
    diagonal = jnp.where(unit(K), gram, 0.0)
    along = lax.rsqrt(jnp.sum(diagonal, axis=0, keepdims=True))
    work[...] = gram * along * lax.rsqrt(jnp.sum(diagonal, axis=1, keepdims=True))

    def block(b, _):
        at = pl.multiple_of(b * B, B)
        low = leaf(work[pl.ds(at, B), pl.ds(at, B)])
        work[pl.ds(at, B), pl.ds(at, B)] = jnp.where(unit(B), 1.0, 0.0)
        top = dot(low, work[pl.ds(at, B), :], 1, 0)
        lane = lax.broadcasted_iota(jnp.int32, (B, K), 1)
        out_ref[pl.ds(at, B), :] = jnp.where(lane < at + B, top, 0.0) * along
        for i in range(1, K // B):
            @pl.when(i > b)
            def _():
                to = B * i
                work[to:to + B, pl.ds(at, B)] = jnp.zeros((B, B), jnp.float32)
                work[to:to + B, :] = work[to:to + B, :] - dot(top[:, to:to + B], top, 0, 0)
        return 0

    lax.fori_loop(0, K // B, block, 0)


def inverse_factor(gram):
    return pl.pallas_call(
        chol_inverse,
        out_shape=jax.ShapeDtypeStruct((K, K), jnp.float32),
        in_specs=[pl.BlockSpec(memory_space=pltpu.VMEM)],
        out_specs=pl.BlockSpec(memory_space=pltpu.VMEM),
        scratch_shapes=[pltpu.VMEM((K, K), jnp.float32)],
        compiler_params=pltpu.CompilerParams(vmem_limit_bytes=12 * 1024 * 1024),
        cost_estimate=pl.CostEstimate(flops=2 * K ** 3, bytes_accessed=8 * K * K, transcendentals=0),
    )(gram)


def permute(values, where):
    places = [(z, y, x, c) for z in range(8) for y in range(4) for x in range(4) for c in range(2)]
    index = {place: i for i, place in enumerate(places)}
    return lax.ppermute(values, AXES, [(index[p], index[where(*p)]) for p in places])


def other_core(z, y, x, c):
    return z, y, x, 1 - c


def exchange(pieces, axes):
    return lax.all_to_all(pieces, axes, 0, 0, tiled=True)


def copies(values, axes):
    return jnp.broadcast_to(values[None], (lax.axis_size(axes),) + values.shape)


def up(z, y, x, c):
    return z, (y + 1) % 4, x, c


def down(z, y, x, c):
    return z, (y - 1) % 4, x, c


def gather_y(own):
    half = own.shape[0] // 2
    before, after = permute(own, up), permute(own, down)
    far = jnp.concatenate([permute(before[:half], up), permute(after[half:], down)], axis=0)
    return [own, after, far, before]


def gather_y_small(own):
    far = permute(own, lambda z, y, x, c: (z, (y + 2) % 4, x, c))
    rows = own.shape[0]
    out = jnp.zeros((4 * rows, own.shape[1]), own.dtype)
    for step, piece in enumerate([own, permute(own, down), far, permute(own, up)]):
        out = lax.dynamic_update_slice_in_dim(out, piece, lax.rem(lax.axis_index("y") + step, 4) * rows, 0)
    return out


def column_block(z, y, x, c):
    return 2 * x + c, y, z // 2, z % 2


def spread(many, few):
    many, few = lax.optimization_barrier((many, few))
    return lax.all_gather(many, "z", axis=0, tiled=True), few


def basis_rows(basis, width):
    sent = lax.dynamic_slice(basis, (lax.axis_index("core") * 4 * ROWS, width), (4 * ROWS, K - width))
    many = permute(sent, lambda z, y, x, c: (2 * y + c, x, z // 2, z % 2))
    few = permute(basis[:, :width], column_block)
    many, few = spread(many, few)
    return many, gather_y(few)


def middle_rows(rows, width):
    def chunk_place(z, y, x, c):
        chunk = 8 * y + 2 * x + c
        return chunk // 4, chunk % 4, z // 2, z % 2
    many = permute(rows[:, width:], chunk_place)
    few = permute(rows[:, :width], column_block)
    many, few = spread(gather_y_small(many), few)
    return many, gather_y(exchange(copies(few, "z"), "z").reshape(8 * ROWS, width))


def few_step(place, a_ref, *refs):
    pieces, out_ref = refs[:4], refs[4]
    a = a_ref[...].reshape(4 * ROWS, 8 * ROWS)
    for j in range(4):
        @pl.when(pl.program_id(1) == j)
        def _():
            term = jnp.dot(a, pieces[j][...], preferred_element_type=jnp.float32).reshape(out_ref.shape)
            if j == 0:
                out_ref[...] = term
            else:
                out_ref[...] += term


def product_few(factor, pieces):
    core = lax.axis_index("core")
    width = pieces[0].shape[1]
    place = jnp.stack([lax.axis_index("y"), core]).astype(jnp.int32)
    return pl.pallas_call(
        few_step,
        out_shape=jax.ShapeDtypeStruct((2, 4, ROWS, width), jnp.float32),
        grid_spec=pltpu.PrefetchScalarGridSpec(
            num_scalar_prefetch=1,
            grid=(2, 4),
            in_specs=[
                pl.BlockSpec((4, None, ROWS, 8 * ROWS),
                             lambda h, q, place: (0, lax.rem(place[1] + 1 + h, 2), 0, lax.rem(place[0] + q, 4))),
            ] + [pl.BlockSpec((8 * ROWS, width), lambda h, q, place: (0, 0))] * 4,
            out_specs=pl.BlockSpec((None, 4, ROWS, width), lambda h, q, place: (h, 0, 0, 0)),
        ),
        compiler_params=pltpu.CompilerParams(vmem_limit_bytes=16 * 1024 * 1024),
        cost_estimate=pl.CostEstimate(flops=2 * 8 * ROWS * M // 8 * width, bytes_accessed=8 * 1024 * 1024, transcendentals=0),
    )(place, factor.reshape(4, 2, ROWS, 32 * ROWS), *pieces)


def many_step(place, a_ref, b_ref, *refs):
    step = pl.program_id(0)
    a = a_ref[...].reshape(4 * ROWS, 8 * ROWS)
    out_ref = refs[-1]
    if len(refs) > 1:
        pieces, out_ref, rows_ref = refs[:4], refs[4], refs[5]
        few = pieces[0].shape[1]
        rows_ref[:, few:] = b_ref[...]
        for j in range(4):
            @pl.when(lax.rem(place[1] + j, 4) == step)
            def _():
                rows_ref[:, :few] = pieces[j][...]
    term = jnp.dot(a, b_ref[...], preferred_element_type=jnp.float32).reshape(out_ref.shape)

    @pl.when(step == 0)
    def _():
        out_ref[...] = term

    @pl.when(step > 0)
    def _():
        out_ref[...] += term


def product_many(factor, many, core, pieces=()):
    width = many.shape[1]
    place = jnp.stack([core, lax.axis_index("y")]).astype(jnp.int32)
    out_shape = [jax.ShapeDtypeStruct((4, ROWS, width), jnp.float32)]
    out_specs = [pl.BlockSpec((4, ROWS, width), lambda q, place: (0, 0, 0))]
    if pieces:
        out_shape.append(jax.ShapeDtypeStruct((32 * ROWS, K), jnp.bfloat16))
        out_specs.append(pl.BlockSpec((8 * ROWS, K), lambda q, place: (q, 0)))
    return pl.pallas_call(
        many_step,
        out_shape=out_shape,
        grid_spec=pltpu.PrefetchScalarGridSpec(
            num_scalar_prefetch=1,
            grid=(4,),
            in_specs=[
                pl.BlockSpec((4, None, ROWS, 8 * ROWS), lambda q, place: (0, place[0], 0, q)),
                pl.BlockSpec((8 * ROWS, width), lambda q, place: (q, 0)),
            ] + [pl.BlockSpec((8 * ROWS, K - width), lambda q, place: (0, 0))] * len(pieces),
            out_specs=out_specs,
        ),
        compiler_params=pltpu.CompilerParams(vmem_limit_bytes=16 * 1024 * 1024),
        cost_estimate=pl.CostEstimate(flops=2 * 4 * ROWS * M // 8 * (width), bytes_accessed=8 * 1024 * 1024, transcendentals=0),
    )(place, factor.reshape(4, 2, ROWS, 32 * ROWS), many, *pieces)


def summed_product(factor, many, pieces, keep):
    core = lax.axis_index("core")
    both = product_few(factor, pieces)
    few = both[1] + permute(both[0], other_core)
    many, few = lax.optimization_barrier((many, few))
    came = permute(product_many(factor, many, 1 - core)[0], other_core)
    mine = product_many(factor, many, core, pieces if keep else [])
    total = jnp.concatenate([few, mine[0] + came], axis=2)
    return jnp.sum(exchange(total, "x"), axis=0), mine[-1]


def gram_inverse(values):
    gram = dot(values, values, 0, 0)
    core = lax.axis_index("core")
    half = lambda which: lax.dynamic_slice_in_dim(gram, which * HALF, HALF, 0)
    share = half(core) + permute(half(1 - core), other_core)
    share = jnp.sum(exchange(share.reshape(16, HALF // 16, K), ("y", "x")), axis=0)
    share = jnp.sum(exchange(copies(share, "z"), "z"), axis=0)
    share = exchange(copies(share, ("y", "x")), ("y", "x")).reshape(HALF, K)
    came = permute(share, other_core)
    first = jnp.where(core == 0, share, came)
    second = jnp.where(core == 0, came, share)
    return inverse_factor(jnp.concatenate([first, second], axis=0))


def shards(factor, basis):
    scale = math.sqrt(M)
    first, _ = summed_product(factor, *basis_rows(basis, FEW_FIRST), False)
    middle = (dot(first, gram_inverse(first), 1, 1) * scale).astype(jnp.bfloat16)
    second, column_basis = summed_product(factor, *middle_rows(middle, FEW_SECOND), True)
    return dot(second, gram_inverse(second), 1, 1) * scale, column_basis


def solution(mesh):
    fine = jax.sharding.Mesh(mesh.devices.reshape(SIZES), AXES)
    return jax.shard_map(
        shards,
        mesh=fine,
        in_specs=(P(("z", "y"), ("x", "core")), P(("z", "y"), None)),
        out_specs=(P(AXES, None), P(("x", "core"), None)),
        check_vma=False,
    )
```

```python
import math

import jax
import jax.numpy as jnp
from jax import lax
from jax.experimental import pallas as pl
from jax.experimental.pallas import tpu as pltpu
from jax.sharding import PartitionSpec as P

M = 28672
K = 512
B = 128
R = 8
AXES = ("z", "y", "x", "core")
SIZES = (8, 4, 4, 2)
HALF = K // 2
FEW = 128
ROWS = M // 256


def dot(a, b, ca, cb):
    return lax.dot_general(a, b, (((ca,), (cb,)), ((), ())), precision=lax.Precision.HIGHEST,
                           preferred_element_type=jnp.float32)


def reciprocal_rows(top, at, lane, sub):
    wide = [jnp.broadcast_to(top[:, at + j:at + j + 1], (R, B)) for j in range(R)]
    e = {(i, j): jnp.broadcast_to(wide[j][i:i + 1, :], (R, B)) for i in range(R) for j in range(i + 1)}
    inside = (lane >= at) & (lane < at + R)
    rhs = jnp.where(inside, jnp.where(lane - at == sub, 1.0, 0.0), top)
    row = [jnp.broadcast_to(rhs[i:i + 1, :], (R, B)) for i in range(R)]
    ratio, solved, final = {}, [None] * R, [None] * R
    for k in range(0, R, 2):
        a, b, c = e[k, k], e[k + 1, k], e[k + 1, k + 1]
        det = a * c - b * b
        over = 1.0 / det
        for i in range(k + 2, R):
            ratio[i, k] = (e[i, k] * c - e[i, k + 1] * b) * over
            ratio[i, k + 1] = (e[i, k + 1] * a - e[i, k] * b) * over
        for i in range(k + 2, R):
            for j in range(k + 2, i + 1):
                e[i, j] = e[i, j] - (ratio[i, k] * e[j, k] + ratio[i, k + 1] * e[j, k + 1])
            row[i] = row[i] - (ratio[i, k] * row[k] + ratio[i, k + 1] * row[k + 1])
        solved[k] = (c * row[k] - b * row[k + 1]) * over
        solved[k + 1] = (a * row[k + 1] - b * row[k]) * over
        root = lax.rsqrt(a)
        final[k] = row[k] * root
        final[k + 1] = (row[k + 1] - (b * root) * final[k]) * (lax.rsqrt(det) * (a * root))
    back = [None] * R
    for k in reversed(range(R)):
        z = solved[k]
        for i in reversed(range(k + 2 - k % 2, R)):
            z = z - ratio[i, k] * back[i]
        back[k] = z
    out = final[0]
    for k in range(1, R):
        out = jnp.where(sub == k, final[k], out)
    return jnp.where(lane < at + R, out, 0.0), back, inside


def leaf(block):
    n = B // R
    w = [block[R * i:R * i + R, :] for i in range(n)]
    lane = lax.broadcasted_iota(jnp.int32, (R, B), 1)
    sub = lax.broadcasted_iota(jnp.int32, (R, B), 0)
    done = []
    for p in range(n):
        at = R * p
        rows, back, inside = reciprocal_rows(w[p], at, lane, sub)
        done.append(rows)
        for i in range(p + 1, n):
            new = jnp.where(inside, 0.0, w[i])
            for j in reversed(range(R)):
                new = new - jnp.broadcast_to(w[i][:, at + j:at + j + 1], (R, B)) * back[j]
            w[i] = new
    return jnp.concatenate(done, axis=0)


def unit(n):
    return lax.broadcasted_iota(jnp.int32, (n, n), 0) == lax.broadcasted_iota(jnp.int32, (n, n), 1)


def chol_inverse(gram_ref, out_ref, work):
    gram = gram_ref[...]
    diagonal = jnp.where(unit(K), gram, 0.0)
    along = lax.rsqrt(jnp.sum(diagonal, axis=0, keepdims=True))
    work[...] = gram * along * lax.rsqrt(jnp.sum(diagonal, axis=1, keepdims=True))

    def block(b, _):
        at = pl.multiple_of(b * B, B)
        low = leaf(work[pl.ds(at, B), pl.ds(at, B)])
        work[pl.ds(at, B), pl.ds(at, B)] = jnp.where(unit(B), 1.0, 0.0)
        top = dot(low, work[pl.ds(at, B), :], 1, 0)
        lane = lax.broadcasted_iota(jnp.int32, (B, K), 1)
        out_ref[pl.ds(at, B), :] = jnp.where(lane < at + B, top, 0.0) * along
        for i in range(1, K // B):
            @pl.when(i > b)
            def _():
                to = B * i
                work[to:to + B, pl.ds(at, B)] = jnp.zeros((B, B), jnp.float32)
                work[to:to + B, :] = work[to:to + B, :] - dot(top[:, to:to + B], top, 0, 0)
        return 0

    lax.fori_loop(0, K // B, block, 0)


def inverse_factor(gram):
    return pl.pallas_call(
        chol_inverse,
        out_shape=jax.ShapeDtypeStruct((K, K), jnp.float32),
        in_specs=[pl.BlockSpec(memory_space=pltpu.VMEM)],
        out_specs=pl.BlockSpec(memory_space=pltpu.VMEM),
        scratch_shapes=[pltpu.VMEM((K, K), jnp.float32)],
        compiler_params=pltpu.CompilerParams(vmem_limit_bytes=12 * 1024 * 1024),
        cost_estimate=pl.CostEstimate(flops=2 * K ** 3, bytes_accessed=8 * K * K, transcendentals=0),
    )(gram)


def permute(values, where):
    places = [(z, y, x, c) for z in range(8) for y in range(4) for x in range(4) for c in range(2)]
    index = {place: i for i, place in enumerate(places)}
    return lax.ppermute(values, AXES, [(index[p], index[where(*p)]) for p in places])


def other_core(z, y, x, c):
    return z, y, x, 1 - c


def exchange(pieces, axes):
    return lax.all_to_all(pieces, axes, 0, 0, tiled=True)


def copies(values, axes):
    return jnp.broadcast_to(values[None], (lax.axis_size(axes),) + values.shape)


def up(z, y, x, c):
    return z, (y + 1) % 4, x, c


def down(z, y, x, c):
    return z, (y - 1) % 4, x, c


def gather_y(own):
    half = own.shape[0] // 2
    before, after = permute(own, up), permute(own, down)
    far = jnp.concatenate([permute(before[:half], up), permute(after[half:], down)], axis=0)
    return [own, after, far, before]


def gather_y_small(own):
    far = permute(own, lambda z, y, x, c: (z, (y + 2) % 4, x, c))
    rows = own.shape[0]
    out = jnp.zeros((4 * rows, own.shape[1]), own.dtype)
    for step, piece in enumerate([own, permute(own, down), far, permute(own, up)]):
        out = lax.dynamic_update_slice_in_dim(out, piece, lax.rem(lax.axis_index("y") + step, 4) * rows, 0)
    return out


def chunk_place(z, y, x, c):
    chunk = 8 * y + 2 * x + c
    return chunk // 4, chunk % 4, z // 2, z % 2


def gathered_rows(rows):
    own = permute(rows, chunk_place)
    many, few = lax.optimization_barrier((gather_y_small(own[:, FEW:]), own[:, :FEW]))
    return lax.all_gather(many, "z", axis=0, tiled=True), gather_y(exchange(copies(few, "z"), "z"))


def few_step(place, a_ref, *refs):
    pieces, out_ref, rows_ref = refs[:4], refs[4], refs[5]
    step = pl.program_id(1)

    @pl.when((pl.program_id(0) == 0) & (step == 0))
    def _():
        for j in range(4):
            rows_ref[:, lax.rem(place[0] + j, 4)] = pieces[j][...]

    a = a_ref[...].reshape(4 * ROWS, 8 * ROWS)
    b = rows_ref[pl.ds(2 * step, 2)].reshape(8 * ROWS, FEW)
    term = jnp.dot(a, b, preferred_element_type=jnp.float32).reshape(out_ref.shape)

    @pl.when(step == 0)
    def _():
        out_ref[...] = term

    @pl.when(step > 0)
    def _():
        out_ref[...] += term


def product_few(factor, pieces):
    place = jnp.stack([lax.axis_index("y"), lax.axis_index("core")]).astype(jnp.int32)
    return pl.pallas_call(
        few_step,
        out_shape=[
            jax.ShapeDtypeStruct((2, 4, ROWS, FEW), jnp.float32),
            jax.ShapeDtypeStruct((8, 4, ROWS, FEW), jnp.bfloat16),
        ],
        grid_spec=pltpu.PrefetchScalarGridSpec(
            num_scalar_prefetch=1,
            grid=(2, 4),
            in_specs=[
                pl.BlockSpec((4, None, ROWS, 8 * ROWS), lambda h, q, place: (0, lax.rem(place[1] + 1 + h, 2), 0, q)),
            ] + [pl.BlockSpec((8, ROWS, FEW), lambda h, q, place: (0, 0, 0))] * 4,
            out_specs=[
                pl.BlockSpec((None, 4, ROWS, FEW), lambda h, q, place: (h, 0, 0, 0)),
                pl.BlockSpec((8, 4, ROWS, FEW), lambda h, q, place: (0, 0, 0, 0)),
            ],
        ),
        compiler_params=pltpu.CompilerParams(vmem_limit_bytes=16 * 1024 * 1024),
        cost_estimate=pl.CostEstimate(flops=2 * 8 * ROWS * M // 8 * FEW, bytes_accessed=8 * 1024 * 1024, transcendentals=0),
    )(place, factor.reshape(4, 2, ROWS, 32 * ROWS), *pieces)


def many_step(place, a_ref, b_ref, *refs):
    step = pl.program_id(0)
    a = a_ref[...].reshape(4 * ROWS, 8 * ROWS)
    out_ref = refs[-1]
    if len(refs) > 1:
        few_ref, out_ref, rows_ref = refs
        rows_ref[:, :FEW] = few_ref[...]
        rows_ref[:, FEW:] = b_ref[...]
    term = jnp.dot(a, b_ref[...], preferred_element_type=jnp.float32).reshape(out_ref.shape)

    @pl.when(step == 0)
    def _():
        out_ref[...] = term

    @pl.when(step > 0)
    def _():
        out_ref[...] += term


def product_many(factor, many, core, few=None):
    operands = [many] if few is None else [many, few]
    out_shape = [jax.ShapeDtypeStruct((4, ROWS, K - FEW), jnp.float32)]
    out_specs = [pl.BlockSpec((4, ROWS, K - FEW), lambda q, place: (0, 0, 0))]
    if few is not None:
        out_shape.append(jax.ShapeDtypeStruct((32 * ROWS, K), jnp.bfloat16))
        out_specs.append(pl.BlockSpec((8 * ROWS, K), lambda q, place: (q, 0)))
    return pl.pallas_call(
        many_step,
        out_shape=out_shape,
        grid_spec=pltpu.PrefetchScalarGridSpec(
            num_scalar_prefetch=1,
            grid=(4,),
            in_specs=[pl.BlockSpec((4, None, ROWS, 8 * ROWS), lambda q, place: (0, place[0], 0, q))]
            + [pl.BlockSpec((8 * ROWS, operand.shape[1]), lambda q, place: (q, 0)) for operand in operands],
            out_specs=out_specs,
        ),
        compiler_params=pltpu.CompilerParams(vmem_limit_bytes=16 * 1024 * 1024),
        cost_estimate=pl.CostEstimate(flops=2 * 4 * ROWS * M // 8 * (K - FEW), bytes_accessed=8 * 1024 * 1024, transcendentals=0),
    )(core.astype(jnp.int32).reshape(1), factor.reshape(4, 2, ROWS, 32 * ROWS), *operands)


def summed_product(factor, rows, keep):
    core = lax.axis_index("core")
    many, pieces = gathered_rows(rows)
    both, ordered = product_few(factor, pieces)
    few = both[1] + permute(both[0], other_core)
    many, few = lax.optimization_barrier((many, few))
    came = permute(product_many(factor, many, 1 - core)[0], other_core)
    mine = product_many(factor, many, core, ordered.reshape(32 * ROWS, FEW) if keep else None)
    total = jnp.concatenate([few, mine[0] + came], axis=2)
    return jnp.sum(exchange(total, "x"), axis=0), mine[-1]


def gram_inverse(values):
    gram = dot(values, values, 0, 0)
    core = lax.axis_index("core")
    half = lambda which: lax.dynamic_slice_in_dim(gram, which * HALF, HALF, 0)
    share = half(core) + permute(half(1 - core), other_core)
    share = jnp.sum(exchange(share.reshape(16, HALF // 16, K), ("y", "x")), axis=0)
    share = jnp.sum(exchange(copies(share, "z"), "z"), axis=0)
    share = exchange(copies(share, ("y", "x")), ("y", "x")).reshape(HALF, K)
    came = permute(share, other_core)
    first = jnp.where(core == 0, share, came)
    second = jnp.where(core == 0, came, share)
    return inverse_factor(jnp.concatenate([first, second], axis=0))


def shards(factor, basis):
    scale = math.sqrt(M)
    own = lax.dynamic_slice_in_dim(basis, lax.axis_index(("x", "core")) * ROWS, ROWS, 0)
    first, _ = summed_product(factor, own, False)
    middle = (dot(first, gram_inverse(first), 1, 1) * scale).astype(jnp.bfloat16)
    second, column_basis = summed_product(factor, middle, True)
    return dot(second, gram_inverse(second), 1, 1) * scale, column_basis


def solution(mesh):
    fine = jax.sharding.Mesh(mesh.devices.reshape(SIZES), AXES)
    return jax.shard_map(
        shards,
        mesh=fine,
        in_specs=(P(("z", "y"), ("x", "core")), P(("z", "y"), None)),
        out_specs=(P(AXES, None), P(("x", "core"), None)),
        check_vma=False,
    )
```

```python
import math

import jax
import jax.numpy as jnp
from jax import lax
from jax.experimental import pallas as pl
from jax.experimental.pallas import tpu as pltpu
from jax.sharding import PartitionSpec as P

M = 28672
K = 512
B = 128
R = 8
AXES = ("z", "y", "x", "core")
SIZES = (8, 4, 4, 2)
HALF = K // 2
FEW = 128
ROWS = M // 256


def dot(a, b, ca, cb):
    return lax.dot_general(a, b, (((ca,), (cb,)), ((), ())), precision=lax.Precision.HIGHEST,
                           preferred_element_type=jnp.float32)


def reciprocal_rows(top, at, lane, sub):
    wide = [jnp.broadcast_to(top[:, at + j:at + j + 1], (R, B)) for j in range(R)]
    e = {(i, j): jnp.broadcast_to(wide[j][i:i + 1, :], (R, B)) for i in range(R) for j in range(i + 1)}
    inside = (lane >= at) & (lane < at + R)
    rhs = jnp.where(inside, jnp.where(lane - at == sub, 1.0, 0.0), top)
    row = [jnp.broadcast_to(rhs[i:i + 1, :], (R, B)) for i in range(R)]
    ratio, solved, final = {}, [None] * R, [None] * R
    for k in range(0, R, 2):
        a, b, c = e[k, k], e[k + 1, k], e[k + 1, k + 1]
        det = a * c - b * b
        over = 1.0 / det
        for i in range(k + 2, R):
            ratio[i, k] = (e[i, k] * c - e[i, k + 1] * b) * over
            ratio[i, k + 1] = (e[i, k + 1] * a - e[i, k] * b) * over
        for i in range(k + 2, R):
            for j in range(k + 2, i + 1):
                e[i, j] = e[i, j] - (ratio[i, k] * e[j, k] + ratio[i, k + 1] * e[j, k + 1])
            row[i] = row[i] - (ratio[i, k] * row[k] + ratio[i, k + 1] * row[k + 1])
        solved[k] = (c * row[k] - b * row[k + 1]) * over
        solved[k + 1] = (a * row[k + 1] - b * row[k]) * over
        root = lax.rsqrt(a)
        final[k] = row[k] * root
        final[k + 1] = (row[k + 1] - (b * root) * final[k]) * (lax.rsqrt(det) * (a * root))
    back = [None] * R
    for k in reversed(range(R)):
        z = solved[k]
        for i in reversed(range(k + 2 - k % 2, R)):
            z = z - ratio[i, k] * back[i]
        back[k] = z
    out = final[0]
    for k in range(1, R):
        out = jnp.where(sub == k, final[k], out)
    return jnp.where(lane < at + R, out, 0.0), back, inside


def leaf(block):
    n = B // R
    w = [block[R * i:R * i + R, :] for i in range(n)]
    lane = lax.broadcasted_iota(jnp.int32, (R, B), 1)
    sub = lax.broadcasted_iota(jnp.int32, (R, B), 0)
    done = []
    for p in range(n):
        at = R * p
        rows, back, inside = reciprocal_rows(w[p], at, lane, sub)
        done.append(rows)
        for i in range(p + 1, n):
            new = jnp.where(inside, 0.0, w[i])
            for j in reversed(range(R)):
                new = new - jnp.broadcast_to(w[i][:, at + j:at + j + 1], (R, B)) * back[j]
            w[i] = new
    return jnp.concatenate(done, axis=0)


def unit(n):
    return lax.broadcasted_iota(jnp.int32, (n, n), 0) == lax.broadcasted_iota(jnp.int32, (n, n), 1)


def halves():
    lower = [(i, j) for i in range(K // B) for j in range(i + 1)]
    return lower[:5], lower[5:]


def gram_step(place, parts_ref, sum_ref, packed_ref):
    total = (parts_ref[0] + parts_ref[1]) + (parts_ref[2] + parts_ref[3])
    sum_ref[...] = total
    for half, blocks in enumerate(halves()):
        slot = jnp.where(place[0] == half, 1, 0)
        for at, (i, j) in enumerate(blocks):
            packed_ref[slot, at] = dot(total[:, B * i:B * i + B], total[:, B * j:B * j + B], 0, 0)


def chol_inverse(place, own_ref, came_ref, out_ref, work):
    for half, blocks in enumerate(halves()):
        for at, (i, j) in enumerate(blocks):
            entry = jnp.where(place[0] == half, own_ref[at], came_ref[at])
            work[B * i:B * i + B, B * j:B * j + B] = entry
            if i != j:
                work[B * j:B * j + B, B * i:B * i + B] = entry.T
    gram = work[...]
    diagonal = jnp.where(unit(K), gram, 0.0)
    along = lax.rsqrt(jnp.sum(diagonal, axis=0, keepdims=True))
    work[...] = gram * along * lax.rsqrt(jnp.sum(diagonal, axis=1, keepdims=True))

    def block(b, _):
        at = pl.multiple_of(b * B, B)
        low = leaf(work[pl.ds(at, B), pl.ds(at, B)])
        work[pl.ds(at, B), pl.ds(at, B)] = jnp.where(unit(B), 1.0, 0.0)
        top = dot(low, work[pl.ds(at, B), :], 1, 0)
        lane = lax.broadcasted_iota(jnp.int32, (B, K), 1)
        out_ref[pl.ds(at, B), :] = jnp.where(lane < at + B, top, 0.0) * along
        for i in range(1, K // B):
            @pl.when(i > b)
            def _():
                to = B * i
                work[to:to + B, pl.ds(at, B)] = jnp.zeros((B, B), jnp.float32)
                work[to:to + B, :] = work[to:to + B, :] - dot(top[:, to:to + B], top, 0, 0)
        return 0

    lax.fori_loop(0, K // B, block, 0)


VMEM = pl.BlockSpec(memory_space=pltpu.VMEM)
SMEM = pl.BlockSpec(memory_space=pltpu.SMEM)
HBM = pl.BlockSpec(memory_space=pl.ANY)


def core_place():
    return lax.axis_index("core").astype(jnp.int32).reshape(1)


def summed_gram(place, parts):
    return pl.pallas_call(
        gram_step,
        out_shape=[
            jax.ShapeDtypeStruct((ROWS, K), jnp.float32),
            jax.ShapeDtypeStruct((2, 5, B, B), jnp.float32),
        ],
        in_specs=[SMEM, VMEM],
        out_specs=[VMEM, VMEM],
        compiler_params=pltpu.CompilerParams(vmem_limit_bytes=12 * 1024 * 1024),
        cost_estimate=pl.CostEstimate(flops=2 * ROWS * K * K, bytes_accessed=8 * K * K, transcendentals=0),
    )(place, parts)


def inverse_factor(place, own, came):
    return pl.pallas_call(
        chol_inverse,
        out_shape=jax.ShapeDtypeStruct((K, K), jnp.float32),
        in_specs=[SMEM, VMEM, VMEM],
        out_specs=VMEM,
        scratch_shapes=[pltpu.VMEM((K, K), jnp.float32)],
        compiler_params=pltpu.CompilerParams(vmem_limit_bytes=12 * 1024 * 1024),
        cost_estimate=pl.CostEstimate(flops=2 * K ** 3, bytes_accessed=8 * K * K, transcendentals=0),
    )(place, own, came)


def permute(values, where):
    places = [(z, y, x, c) for z in range(8) for y in range(4) for x in range(4) for c in range(2)]
    index = {place: i for i, place in enumerate(places)}
    return lax.ppermute(values, AXES, [(index[p], index[where(*p)]) for p in places])


def other_core(z, y, x, c):
    return z, y, x, 1 - c


def exchange(pieces, axes):
    return lax.all_to_all(pieces, axes, 0, 0, tiled=True)


def copies(values, axes):
    return jnp.broadcast_to(values[None], (lax.axis_size(axes),) + values.shape)


def up(z, y, x, c):
    return z, (y + 1) % 4, x, c


def down(z, y, x, c):
    return z, (y - 1) % 4, x, c


def gather_y(own):
    half = own.shape[0] // 2
    before, after = permute(own, up), permute(own, down)
    far = jnp.concatenate([permute(before[:half], up), permute(after[half:], down)], axis=0)
    return [own, after, far, before]


def gather_y_small(own):
    far = permute(own, lambda z, y, x, c: (z, (y + 2) % 4, x, c))
    rows = own.shape[0]
    out = jnp.zeros((4 * rows, own.shape[1]), own.dtype)
    for step, piece in enumerate([own, permute(own, down), far, permute(own, up)]):
        out = lax.dynamic_update_slice_in_dim(out, piece, lax.rem(lax.axis_index("y") + step, 4) * rows, 0)
    return out


def chunk_place(z, y, x, c):
    chunk = 8 * y + 2 * x + c
    return chunk // 4, chunk % 4, z // 2, z % 2


def gathered_rows(rows):
    own = permute(rows, chunk_place)
    many, few = lax.optimization_barrier((gather_y_small(own[:, FEW:]), own[:, :FEW]))
    return lax.all_gather(many, "z", axis=0, tiled=True), gather_y(exchange(copies(few, "z"), "z"))


def few_step(place, a_ref, *refs):
    pieces, out_ref, rows_ref = refs[:4], refs[4], refs[5]
    step = pl.program_id(1)

    @pl.when((pl.program_id(0) == 0) & (step == 0))
    def _():
        for j in range(4):
            rows_ref[:, lax.rem(place[0] + j, 4)] = pieces[j][...]

    a = a_ref[...].reshape(4 * ROWS, 8 * ROWS)
    b = rows_ref[pl.ds(2 * step, 2)].reshape(8 * ROWS, FEW)
    term = jnp.dot(a, b, preferred_element_type=jnp.float32).reshape(out_ref.shape)

    @pl.when(step == 0)
    def _():
        out_ref[...] = term

    @pl.when(step > 0)
    def _():
        out_ref[...] += term


def product_few(factor, pieces):
    place = jnp.stack([lax.axis_index("y"), lax.axis_index("core")]).astype(jnp.int32)
    return pl.pallas_call(
        few_step,
        out_shape=[
            jax.ShapeDtypeStruct((2, 4, ROWS, FEW), jnp.float32),
            jax.ShapeDtypeStruct((8, 4, ROWS, FEW), jnp.bfloat16),
        ],
        grid_spec=pltpu.PrefetchScalarGridSpec(
            num_scalar_prefetch=1,
            grid=(2, 4),
            in_specs=[
                pl.BlockSpec((4, None, ROWS, 8 * ROWS), lambda h, q, place: (0, lax.rem(place[1] + 1 + h, 2), 0, q)),
            ] + [pl.BlockSpec((8, ROWS, FEW), lambda h, q, place: (0, 0, 0))] * 4,
            out_specs=[
                pl.BlockSpec((None, 4, ROWS, FEW), lambda h, q, place: (h, 0, 0, 0)),
                pl.BlockSpec((8, 4, ROWS, FEW), lambda h, q, place: (0, 0, 0, 0)),
            ],
        ),
        compiler_params=pltpu.CompilerParams(vmem_limit_bytes=16 * 1024 * 1024),
        cost_estimate=pl.CostEstimate(flops=2 * 8 * ROWS * M // 8 * FEW, bytes_accessed=8 * 1024 * 1024, transcendentals=0),
    )(place, factor.reshape(4, 2, ROWS, 32 * ROWS), *pieces)


def many_step(place, a_ref, b_ref, *refs):
    few_ref = rows_ref = None
    if len(refs) > 8:
        few_ref, theirs_ref, mine_ref, rows_ref = refs[:4]
    else:
        theirs_ref, mine_ref = refs[:2]
    a_held, b_held, total, a_sem, b_sem, rows_sem = refs[-6:]
    steps, deep = a_held.shape[0], a_held.shape[2]
    inward = [
        (
            pltpu.make_async_copy(a_ref.at[:, pl.ds(q * deep, deep)], a_held.at[q], a_sem.at[q]),
            pltpu.make_async_copy(b_ref.at[pl.ds(q * deep, deep)], b_held.at[q], b_sem.at[q]),
        )
        for q in range(steps)
    ]
    outward = []

    def start(copies):
        for copy in copies:
            copy.start()

    for q in range(steps):
        start(inward[q])
    if rows_ref is not None:
        outward.append(pltpu.make_async_copy(few_ref, rows_ref.at[:, pl.ds(0, FEW)], rows_sem.at[steps]))
        start(outward)
    for q in range(steps):
        for copy in inward[q]:
            copy.wait()
        if rows_ref is not None:
            outward.append(pltpu.make_async_copy(
                b_held.at[q], rows_ref.at[pl.ds(q * deep, deep), pl.ds(FEW, K - FEW)], rows_sem.at[q]))
            start(outward[-1:])
        term = jnp.dot(a_held[q], b_held[q], preferred_element_type=jnp.float32).reshape(total.shape)
        if q == 0:
            total[...] = term
        else:
            total[...] += term
    theirs_ref[...] = total[:, 1 - place[0]]
    mine_ref[...] = total[:, place[0]]
    for copy in outward:
        copy.wait()


def product_many(factor, many, place, few=None):
    steps = 7
    deep = 32 * ROWS // steps
    operands = [factor, many] if few is None else [factor, many, few]
    part = jax.ShapeDtypeStruct((4, ROWS, K - FEW), jnp.float32)
    return pl.pallas_call(
        many_step,
        out_shape=[part, part] + [jax.ShapeDtypeStruct((32 * ROWS, K), jnp.bfloat16)] * (len(operands) - 2),
        in_specs=[SMEM, HBM, HBM] + [VMEM] * (len(operands) - 2),
        out_specs=[VMEM, VMEM] + [HBM] * (len(operands) - 2),
        scratch_shapes=[
            pltpu.VMEM((steps, 8 * ROWS, deep), jnp.bfloat16),
            pltpu.VMEM((steps, deep, K - FEW), jnp.bfloat16),
            pltpu.VMEM((4, 2, ROWS, K - FEW), jnp.float32),
            pltpu.SemaphoreType.DMA((steps,)),
            pltpu.SemaphoreType.DMA((steps,)),
            pltpu.SemaphoreType.DMA((steps + 1,)),
        ],
        compiler_params=pltpu.CompilerParams(vmem_limit_bytes=60 * 1024 * 1024),
        cost_estimate=pl.CostEstimate(flops=2 * 8 * ROWS * M // 8 * (K - FEW), bytes_accessed=12 * 1024 * 1024, transcendentals=0),
    )(place, *operands)


def summed_product(factor, rows, keep):
    place = core_place()
    many, pieces = gathered_rows(rows)
    both, ordered = product_few(factor, pieces)
    few = both[1] + permute(both[0], other_core)
    many, few = lax.optimization_barrier((many, few))
    theirs, mine, *rest = product_many(factor, many, place, ordered.reshape(32 * ROWS, FEW) if keep else None)
    total = jnp.concatenate([few, mine + permute(theirs, other_core)], axis=2)
    return summed_gram(place, exchange(total, "x")), rest


def gram_inverse(packed):
    share = packed[1] + permute(packed[0], other_core)
    share = jnp.sum(exchange(share.reshape(16, 5 * B // 16, B), ("y", "x")), axis=0)
    share = jnp.sum(exchange(copies(share, "z"), "z"), axis=0)
    share = exchange(copies(share, ("y", "x")), ("y", "x")).reshape(5, B, B)
    return inverse_factor(core_place(), share, permute(share, other_core))


def shards(factor, basis):
    scale = math.sqrt(M)
    own = lax.dynamic_slice_in_dim(basis, lax.axis_index(("x", "core")) * ROWS, ROWS, 0)
    (first, packed), _ = summed_product(factor, own, False)
    middle = (dot(first, gram_inverse(packed), 1, 1) * scale).astype(jnp.bfloat16)
    (second, packed), (column_basis,) = summed_product(factor, middle, True)
    return dot(second, gram_inverse(packed), 1, 1) * scale, column_basis


def solution(mesh):
    fine = jax.sharding.Mesh(mesh.devices.reshape(SIZES), AXES)
    return jax.shard_map(
        shards,
        mesh=fine,
        in_specs=(P(("z", "y"), ("x", "core")), P(("z", "y"), None)),
        out_specs=(P(AXES, None), P(("x", "core"), None)),
        check_vma=False,
    )
```

```python
import math

import jax
import jax.numpy as jnp
from jax import lax
from jax.experimental import pallas as pl
from jax.experimental.pallas import tpu as pltpu
from jax.sharding import PartitionSpec as P

M = 28672
K = 512
B = 128
R = 8
AXES = ("z", "y", "x", "core")
SIZES = (8, 4, 4, 2)
HALF = K // 2
FEW = 256
ROWS = M // 256


def dot(a, b, ca, cb):
    return lax.dot_general(a, b, (((ca,), (cb,)), ((), ())), precision=lax.Precision.HIGHEST,
                           preferred_element_type=jnp.float32)


def reciprocal_rows(top, at, lane, sub):
    wide = [jnp.broadcast_to(top[:, at + j:at + j + 1], (R, B)) for j in range(R)]
    e = {(i, j): jnp.broadcast_to(wide[j][i:i + 1, :], (R, B)) for i in range(R) for j in range(i + 1)}
    inside = (lane >= at) & (lane < at + R)
    rhs = jnp.where(inside, jnp.where(lane - at == sub, 1.0, 0.0), top)
    row = [jnp.broadcast_to(rhs[i:i + 1, :], (R, B)) for i in range(R)]
    ratio, solved, final = {}, [None] * R, [None] * R
    for k in range(0, R, 2):
        a, b, c = e[k, k], e[k + 1, k], e[k + 1, k + 1]
        det = a * c - b * b
        over = 1.0 / det
        for i in range(k + 2, R):
            ratio[i, k] = (e[i, k] * c - e[i, k + 1] * b) * over
            ratio[i, k + 1] = (e[i, k + 1] * a - e[i, k] * b) * over
        for i in range(k + 2, R):
            for j in range(k + 2, i + 1):
                if i < k + 4:
                    one = (e[i, k] * c - e[i, k + 1] * b) * e[j, k]
                    two = (e[i, k + 1] * a - e[i, k] * b) * e[j, k + 1]
                    e[i, j] = e[i, j] - (one + two) * over
                else:
                    e[i, j] = e[i, j] - (ratio[i, k] * e[j, k] + ratio[i, k + 1] * e[j, k + 1])
            row[i] = row[i] - (ratio[i, k] * row[k] + ratio[i, k + 1] * row[k + 1])
        solved[k] = (c * row[k] - b * row[k + 1]) * over
        solved[k + 1] = (a * row[k + 1] - b * row[k]) * over
        root = lax.rsqrt(a)
        final[k] = row[k] * root
        final[k + 1] = (row[k + 1] - (b * root) * final[k]) * (lax.rsqrt(det) * (a * root))
    back = [None] * R
    for k in reversed(range(R)):
        z = solved[k]
        for i in reversed(range(k + 2 - k % 2, R)):
            z = z - ratio[i, k] * back[i]
        back[k] = z
    out = final[0]
    for k in range(1, R):
        out = jnp.where(sub == k, final[k], out)
    return jnp.where(lane < at + R, out, 0.0), back, inside


def leaf(block):
    n = B // R
    w = [block[R * i:R * i + R, :] for i in range(n)]
    lane = lax.broadcasted_iota(jnp.int32, (R, B), 1)
    sub = lax.broadcasted_iota(jnp.int32, (R, B), 0)
    done = []
    for p in range(n):
        at = R * p
        rows, back, inside = reciprocal_rows(w[p], at, lane, sub)
        done.append(rows)
        for i in range(p + 1, n):
            new = jnp.where(inside, 0.0, w[i])
            for j in reversed(range(R)):
                new = new - jnp.broadcast_to(w[i][:, at + j:at + j + 1], (R, B)) * back[j]
            w[i] = new
    return jnp.concatenate(done, axis=0)


def unit(n):
    return lax.broadcasted_iota(jnp.int32, (n, n), 0) == lax.broadcasted_iota(jnp.int32, (n, n), 1)


def halves():
    lower = [(i, j) for i in range(K // B) for j in range(i + 1)]
    return lower[:5], lower[5:]


def gram_step(place, parts_ref, sum_ref, packed_ref):
    total = (parts_ref[0] + parts_ref[1]) + (parts_ref[2] + parts_ref[3])
    sum_ref[...] = total
    for half, blocks in enumerate(halves()):
        slot = jnp.where(place[0] == half, 1, 0)
        for at, (i, j) in enumerate(blocks):
            packed_ref[slot, at] = dot(total[:, B * i:B * i + B], total[:, B * j:B * j + B], 0, 0)


def chol_inverse(place, own_ref, came_ref, out_ref, work):
    for half, blocks in enumerate(halves()):
        for at, (i, j) in enumerate(blocks):
            entry = jnp.where(place[0] == half, own_ref[at], came_ref[at])
            work[B * i:B * i + B, B * j:B * j + B] = entry
            if i != j:
                work[B * j:B * j + B, B * i:B * i + B] = entry.T
    gram = work[...]
    diagonal = jnp.where(unit(K), gram, 0.0)
    along = lax.rsqrt(jnp.sum(diagonal, axis=0, keepdims=True))
    work[...] = gram * along * lax.rsqrt(jnp.sum(diagonal, axis=1, keepdims=True))

    def block(b, _):
        at = pl.multiple_of(b * B, B)
        low = leaf(work[pl.ds(at, B), pl.ds(at, B)])
        work[pl.ds(at, B), pl.ds(at, B)] = jnp.where(unit(B), 1.0, 0.0)
        top = dot(low, work[pl.ds(at, B), :], 1, 0)
        lane = lax.broadcasted_iota(jnp.int32, (B, K), 1)
        out_ref[pl.ds(at, B), :] = jnp.where(lane < at + B, top, 0.0) * along
        for i in range(1, K // B):
            @pl.when(i > b)
            def _():
                to = B * i
                work[to:to + B, pl.ds(at, B)] = jnp.zeros((B, B), jnp.float32)
                work[to:to + B, :] = work[to:to + B, :] - dot(top[:, to:to + B], top, 0, 0)
        return 0

    lax.fori_loop(0, K // B, block, 0)


VMEM = pl.BlockSpec(memory_space=pltpu.VMEM)
SMEM = pl.BlockSpec(memory_space=pltpu.SMEM)
HBM = pl.BlockSpec(memory_space=pl.ANY)


def core_place():
    return lax.axis_index("core").astype(jnp.int32).reshape(1)


def summed_gram(place, parts):
    return pl.pallas_call(
        gram_step,
        out_shape=[
            jax.ShapeDtypeStruct((ROWS, K), jnp.float32),
            jax.ShapeDtypeStruct((2, 5, B, B), jnp.float32),
        ],
        in_specs=[SMEM, VMEM],
        out_specs=[VMEM, VMEM],
        compiler_params=pltpu.CompilerParams(vmem_limit_bytes=12 * 1024 * 1024),
        cost_estimate=pl.CostEstimate(flops=2 * ROWS * K * K, bytes_accessed=8 * K * K, transcendentals=0),
    )(place, parts)


def inverse_factor(place, own, came):
    return pl.pallas_call(
        chol_inverse,
        out_shape=jax.ShapeDtypeStruct((K, K), jnp.float32),
        in_specs=[SMEM, VMEM, VMEM],
        out_specs=VMEM,
        scratch_shapes=[pltpu.VMEM((K, K), jnp.float32)],
        compiler_params=pltpu.CompilerParams(vmem_limit_bytes=12 * 1024 * 1024),
        cost_estimate=pl.CostEstimate(flops=2 * K ** 3, bytes_accessed=8 * K * K, transcendentals=0),
    )(place, own, came)


def permute(values, where):
    places = [(z, y, x, c) for z in range(8) for y in range(4) for x in range(4) for c in range(2)]
    index = {place: i for i, place in enumerate(places)}
    return lax.ppermute(values, AXES, [(index[p], index[where(*p)]) for p in places])


def other_core(z, y, x, c):
    return z, y, x, 1 - c


def exchange(pieces, axes):
    return lax.all_to_all(pieces, axes, 0, 0, tiled=True)


def copies(values, axes):
    return jnp.broadcast_to(values[None], (lax.axis_size(axes),) + values.shape)


def up(z, y, x, c):
    return z, (y + 1) % 4, x, c


def down(z, y, x, c):
    return z, (y - 1) % 4, x, c


def gather_y(own):
    half = own.shape[0] // 2
    before, after = permute(own, up), permute(own, down)
    far = jnp.concatenate([permute(before[:half], up), permute(after[half:], down)], axis=0)
    return [own, after, far, before]


def gather_y_small(own):
    far = permute(own, lambda z, y, x, c: (z, (y + 2) % 4, x, c))
    rows = own.shape[0]
    out = jnp.zeros((4 * rows, own.shape[1]), own.dtype)
    for step, piece in enumerate([own, permute(own, down), far, permute(own, up)]):
        out = lax.dynamic_update_slice_in_dim(out, piece, lax.rem(lax.axis_index("y") + step, 4) * rows, 0)
    return out


def chunk_place(z, y, x, c):
    chunk = 8 * y + 2 * x + c
    return chunk // 4, chunk % 4, z // 2, z % 2


def gathered_rows(rows):
    own = permute(rows, chunk_place)
    many, few = gather_y_small(own[:, FEW:]), exchange(copies(own[:, :FEW], "z"), "z")
    many, few = lax.optimization_barrier((many, few))
    return lax.all_gather(many, "z", axis=0, tiled=True), gather_y(few)


def few_step(place, a_ref, *refs):
    pieces, out_ref, rows_ref = refs[:4], refs[4], refs[5]
    step = pl.program_id(1)

    @pl.when((pl.program_id(0) == 0) & (step == 0))
    def _():
        for j in range(4):
            rows_ref[:, lax.rem(place[0] + j, 4)] = pieces[j][...]

    a = a_ref[...].reshape(4 * ROWS, 8 * ROWS)
    b = rows_ref[pl.ds(2 * step, 2)].reshape(8 * ROWS, FEW)
    term = jnp.dot(a, b, preferred_element_type=jnp.float32).reshape(out_ref.shape)

    @pl.when(step == 0)
    def _():
        out_ref[...] = term

    @pl.when(step > 0)
    def _():
        out_ref[...] += term


def product_few(factor, pieces):
    place = jnp.stack([lax.axis_index("y"), lax.axis_index("core")]).astype(jnp.int32)
    return pl.pallas_call(
        few_step,
        out_shape=[
            jax.ShapeDtypeStruct((2, 4, ROWS, FEW), jnp.float32),
            jax.ShapeDtypeStruct((8, 4, ROWS, FEW), jnp.bfloat16),
        ],
        grid_spec=pltpu.PrefetchScalarGridSpec(
            num_scalar_prefetch=1,
            grid=(2, 4),
            in_specs=[
                pl.BlockSpec((4, None, ROWS, 8 * ROWS), lambda h, q, place: (0, lax.rem(place[1] + 1 + h, 2), 0, q)),
            ] + [pl.BlockSpec((8, ROWS, FEW), lambda h, q, place: (0, 0, 0))] * 4,
            out_specs=[
                pl.BlockSpec((None, 4, ROWS, FEW), lambda h, q, place: (h, 0, 0, 0)),
                pl.BlockSpec((8, 4, ROWS, FEW), lambda h, q, place: (0, 0, 0, 0)),
            ],
        ),
        compiler_params=pltpu.CompilerParams(vmem_limit_bytes=16 * 1024 * 1024),
        cost_estimate=pl.CostEstimate(flops=2 * 8 * ROWS * M // 8 * FEW, bytes_accessed=8 * 1024 * 1024, transcendentals=0),
    )(place, factor.reshape(4, 2, ROWS, 32 * ROWS), *pieces)


def many_step(place, a_ref, b_ref, *refs):
    few_ref = rows_ref = None
    if len(refs) > 8:
        few_ref, theirs_ref, mine_ref, rows_ref = refs[:4]
    else:
        theirs_ref, mine_ref = refs[:2]
    a_held, b_held, total, a_sem, b_sem, rows_sem = refs[-6:]
    steps, deep = a_held.shape[0], a_held.shape[2]
    inward = [
        (
            pltpu.make_async_copy(a_ref.at[:, pl.ds(q * deep, deep)], a_held.at[q], a_sem.at[q]),
            pltpu.make_async_copy(b_ref.at[pl.ds(q * deep, deep)], b_held.at[q], b_sem.at[q]),
        )
        for q in range(steps)
    ]
    outward = []

    def start(copies):
        for copy in copies:
            copy.start()

    for q in range(steps):
        start(inward[q])
    if rows_ref is not None:
        outward.append(pltpu.make_async_copy(few_ref, rows_ref.at[:, pl.ds(0, FEW)], rows_sem.at[steps]))
        start(outward)
    for q in range(steps):
        for copy in inward[q]:
            copy.wait()
        if rows_ref is not None:
            outward.append(pltpu.make_async_copy(
                b_held.at[q], rows_ref.at[pl.ds(q * deep, deep), pl.ds(FEW, K - FEW)], rows_sem.at[q]))
            start(outward[-1:])
        term = jnp.dot(a_held[q], b_held[q], preferred_element_type=jnp.float32).reshape(total.shape)
        if q == 0:
            total[...] = term
        else:
            total[...] += term
    theirs_ref[...] = total[:, 1 - place[0]]
    mine_ref[...] = total[:, place[0]]
    for copy in outward:
        copy.wait()


def product_many(factor, many, place, few=None):
    steps = 7
    deep = 32 * ROWS // steps
    operands = [factor, many] if few is None else [factor, many, few]
    part = jax.ShapeDtypeStruct((4, ROWS, K - FEW), jnp.float32)
    return pl.pallas_call(
        many_step,
        out_shape=[part, part] + [jax.ShapeDtypeStruct((32 * ROWS, K), jnp.bfloat16)] * (len(operands) - 2),
        in_specs=[SMEM, HBM, HBM] + [VMEM] * (len(operands) - 2),
        out_specs=[VMEM, VMEM] + [HBM] * (len(operands) - 2),
        scratch_shapes=[
            pltpu.VMEM((steps, 8 * ROWS, deep), jnp.bfloat16),
            pltpu.VMEM((steps, deep, K - FEW), jnp.bfloat16),
            pltpu.VMEM((4, 2, ROWS, K - FEW), jnp.float32),
            pltpu.SemaphoreType.DMA((steps,)),
            pltpu.SemaphoreType.DMA((steps,)),
            pltpu.SemaphoreType.DMA((steps + 1,)),
        ],
        compiler_params=pltpu.CompilerParams(vmem_limit_bytes=60 * 1024 * 1024),
        cost_estimate=pl.CostEstimate(flops=2 * 8 * ROWS * M // 8 * (K - FEW), bytes_accessed=12 * 1024 * 1024, transcendentals=0),
    )(place, *operands)


def summed_product(factor, rows, keep):
    place = core_place()
    many, pieces = gathered_rows(rows)
    both, ordered = product_few(factor, pieces)
    few = both[1] + permute(both[0], other_core)
    many, few = lax.optimization_barrier((many, few))
    theirs, mine, *rest = product_many(factor, many, place, ordered.reshape(32 * ROWS, FEW) if keep else None)
    total = jnp.concatenate([few, mine + permute(theirs, other_core)], axis=2)
    return summed_gram(place, exchange(total, "x")), rest


def gram_inverse(packed):
    share = packed[1] + permute(packed[0], other_core)
    share = jnp.sum(exchange(share.reshape(16, 5 * B // 16, B), ("y", "x")), axis=0)
    share = jnp.sum(exchange(copies(share, "z"), "z"), axis=0)
    share = exchange(copies(share, ("y", "x")), ("y", "x")).reshape(5, B, B)
    return inverse_factor(core_place(), share, permute(share, other_core))


def shards(factor, basis):
    scale = math.sqrt(M)
    own = lax.dynamic_slice_in_dim(basis, lax.axis_index(("x", "core")) * ROWS, ROWS, 0)
    (first, packed), _ = summed_product(factor, own, False)
    middle = (dot(first, gram_inverse(packed), 1, 1) * scale).astype(jnp.bfloat16)
    (second, packed), (column_basis,) = summed_product(factor, middle, True)
    return dot(second, gram_inverse(packed), 1, 1) * scale, column_basis


def solution(mesh):
    fine = jax.sharding.Mesh(mesh.devices.reshape(SIZES), AXES)
    return jax.shard_map(
        shards,
        mesh=fine,
        in_specs=(P(("z", "y"), ("x", "core")), P(("z", "y"), None)),
        out_specs=(P(AXES, None), P(("x", "core"), None)),
        check_vma=False,
    )
```

```python
import math

import jax
import jax.numpy as jnp
from jax import lax
from jax.experimental import pallas as pl
from jax.experimental.pallas import tpu as pltpu
from jax.sharding import PartitionSpec as P

M = 28672
K = 512
B = 128
R = 8
AXES = ("z", "y", "x", "core")
SIZES = (8, 4, 4, 2)
HALF = K // 2
FEW = 128
ROWS = M // 256


def dot(a, b, ca, cb):
    return lax.dot_general(a, b, (((ca,), (cb,)), ((), ())), precision=lax.Precision.HIGHEST,
                           preferred_element_type=jnp.float32)


def reciprocal_rows(top, at, lane, sub):
    wide = [jnp.broadcast_to(top[:, at + j:at + j + 1], (R, B)) for j in range(R)]
    e = {(i, j): jnp.broadcast_to(wide[j][i:i + 1, :], (R, B)) for i in range(R) for j in range(i + 1)}
    inside = (lane >= at) & (lane < at + R)
    rhs = jnp.where(inside, jnp.where(lane - at == sub, 1.0, 0.0), top)
    row = [jnp.broadcast_to(rhs[i:i + 1, :], (R, B)) for i in range(R)]
    ratio, solved, final = {}, [None] * R, [None] * R
    for k in range(0, R, 2):
        a, b, c = e[k, k], e[k + 1, k], e[k + 1, k + 1]
        det = a * c - b * b
        over = 1.0 / det
        for i in range(k + 2, R):
            ratio[i, k] = (e[i, k] * c - e[i, k + 1] * b) * over
            ratio[i, k + 1] = (e[i, k + 1] * a - e[i, k] * b) * over
        for i in range(k + 2, R):
            for j in range(k + 2, i + 1):
                if i < k + 4:
                    one = (e[i, k] * c - e[i, k + 1] * b) * e[j, k]
                    two = (e[i, k + 1] * a - e[i, k] * b) * e[j, k + 1]
                    e[i, j] = e[i, j] - (one + two) * over
                else:
                    e[i, j] = e[i, j] - (ratio[i, k] * e[j, k] + ratio[i, k + 1] * e[j, k + 1])
            row[i] = row[i] - (ratio[i, k] * row[k] + ratio[i, k + 1] * row[k + 1])
        solved[k] = (c * row[k] - b * row[k + 1]) * over
        solved[k + 1] = (a * row[k + 1] - b * row[k]) * over
        root = lax.rsqrt(a)
        final[k] = row[k] * root
        final[k + 1] = (row[k + 1] - (b * root) * final[k]) * (lax.rsqrt(det) * (a * root))
    back = [None] * R
    for k in reversed(range(R)):
        z = solved[k]
        for i in reversed(range(k + 2 - k % 2, R)):
            z = z - ratio[i, k] * back[i]
        back[k] = z
    out = final[0]
    for k in range(1, R):
        out = jnp.where(sub == k, final[k], out)
    return jnp.where(lane < at + R, out, 0.0), back, inside


def leaf(block):
    n = B // R
    w = [block[R * i:R * i + R, :] for i in range(n)]
    lane = lax.broadcasted_iota(jnp.int32, (R, B), 1)
    sub = lax.broadcasted_iota(jnp.int32, (R, B), 0)
    done = []
    for p in range(n):
        at = R * p
        rows, back, inside = reciprocal_rows(w[p], at, lane, sub)
        done.append(rows)
        for i in range(p + 1, n):
            new = jnp.where(inside, 0.0, w[i])
            for j in reversed(range(R)):
                new = new - jnp.broadcast_to(w[i][:, at + j:at + j + 1], (R, B)) * back[j]
            w[i] = new
    return jnp.concatenate(done, axis=0)


def unit(n):
    return lax.broadcasted_iota(jnp.int32, (n, n), 0) == lax.broadcasted_iota(jnp.int32, (n, n), 1)


def halves():
    lower = [(i, j) for i in range(K // B) for j in range(i + 1)]
    return lower[:5], lower[5:]


def gram_step(place, parts_ref, sum_ref, packed_ref):
    total = (parts_ref[0] + parts_ref[1]) + (parts_ref[2] + parts_ref[3])
    sum_ref[...] = total
    for half, blocks in enumerate(halves()):
        slot = jnp.where(place[0] == half, 1, 0)
        for at, (i, j) in enumerate(blocks):
            packed_ref[slot, at] = dot(total[:, B * i:B * i + B], total[:, B * j:B * j + B], 0, 0)


def chol_inverse(place, own_ref, came_ref, out_ref, work):
    for half, blocks in enumerate(halves()):
        for at, (i, j) in enumerate(blocks):
            entry = jnp.where(place[0] == half, own_ref[at], came_ref[at])
            work[B * i:B * i + B, B * j:B * j + B] = entry
            if i != j:
                work[B * j:B * j + B, B * i:B * i + B] = entry.T
    gram = work[...]
    diagonal = jnp.where(unit(K), gram, 0.0)
    along = lax.rsqrt(jnp.sum(diagonal, axis=0, keepdims=True))
    work[...] = gram * along * lax.rsqrt(jnp.sum(diagonal, axis=1, keepdims=True))

    def block(b, _):
        at = pl.multiple_of(b * B, B)
        low = leaf(work[pl.ds(at, B), pl.ds(at, B)])
        work[pl.ds(at, B), pl.ds(at, B)] = jnp.where(unit(B), 1.0, 0.0)
        top = dot(low, work[pl.ds(at, B), :], 1, 0)
        lane = lax.broadcasted_iota(jnp.int32, (B, K), 1)
        out_ref[pl.ds(at, B), :] = jnp.where(lane < at + B, top, 0.0) * along
        for i in range(1, K // B):
            @pl.when(i > b)
            def _():
                to = B * i
                work[to:to + B, pl.ds(at, B)] = jnp.zeros((B, B), jnp.float32)
                work[to:to + B, :] = work[to:to + B, :] - dot(top[:, to:to + B], top, 0, 0)
        return 0

    lax.fori_loop(0, K // B, block, 0)


VMEM = pl.BlockSpec(memory_space=pltpu.VMEM)
SMEM = pl.BlockSpec(memory_space=pltpu.SMEM)
HBM = pl.BlockSpec(memory_space=pl.ANY)


def core_place():
    return lax.axis_index("core").astype(jnp.int32).reshape(1)


def summed_gram(place, parts):
    return pl.pallas_call(
        gram_step,
        out_shape=[
            jax.ShapeDtypeStruct((ROWS, K), jnp.float32),
            jax.ShapeDtypeStruct((2, 5, B, B), jnp.float32),
        ],
        in_specs=[SMEM, VMEM],
        out_specs=[VMEM, VMEM],
        compiler_params=pltpu.CompilerParams(vmem_limit_bytes=12 * 1024 * 1024),
        cost_estimate=pl.CostEstimate(flops=2 * ROWS * K * K, bytes_accessed=8 * K * K, transcendentals=0),
    )(place, parts)


def inverse_factor(place, own, came):
    return pl.pallas_call(
        chol_inverse,
        out_shape=jax.ShapeDtypeStruct((K, K), jnp.float32),
        in_specs=[SMEM, VMEM, VMEM],
        out_specs=VMEM,
        scratch_shapes=[pltpu.VMEM((K, K), jnp.float32)],
        compiler_params=pltpu.CompilerParams(vmem_limit_bytes=12 * 1024 * 1024),
        cost_estimate=pl.CostEstimate(flops=2 * K ** 3, bytes_accessed=8 * K * K, transcendentals=0),
    )(place, own, came)


def permute(values, where):
    places = [(z, y, x, c) for z in range(8) for y in range(4) for x in range(4) for c in range(2)]
    index = {place: i for i, place in enumerate(places)}
    return lax.ppermute(values, AXES, [(index[p], index[where(*p)]) for p in places])


def other_core(z, y, x, c):
    return z, y, x, 1 - c


def exchange(pieces, axes):
    return lax.all_to_all(pieces, axes, 0, 0, tiled=True)


def copies(values, axes):
    return jnp.broadcast_to(values[None], (lax.axis_size(axes),) + values.shape)


def up(z, y, x, c):
    return z, (y + 1) % 4, x, c


def down(z, y, x, c):
    return z, (y - 1) % 4, x, c


def gather_y(own):
    half = own.shape[0] // 2
    before, after = permute(own, up), permute(own, down)
    far = jnp.concatenate([permute(before[:half], up), permute(after[half:], down)], axis=0)
    return [own, after, far, before]


def gather_y_small(own):
    far = permute(own, lambda z, y, x, c: (z, (y + 2) % 4, x, c))
    rows = own.shape[0]
    out = jnp.zeros((4 * rows, own.shape[1]), own.dtype)
    for step, piece in enumerate([own, permute(own, down), far, permute(own, up)]):
        out = lax.dynamic_update_slice_in_dim(out, piece, lax.rem(lax.axis_index("y") + step, 4) * rows, 0)
    return out


def chunk_place(z, y, x, c):
    chunk = 8 * y + 2 * x + c
    return chunk // 4, chunk % 4, z // 2, z % 2


def gathered_rows(few, many):
    many, few = lax.optimization_barrier((many, few))
    return lax.all_gather(many, "z", axis=0, tiled=True), gather_y(exchange(copies(few, "z"), "z"))


def few_step(place, a_ref, *refs):
    pieces, out_ref, rows_ref = refs[:4], refs[4], refs[5]
    step = pl.program_id(1)

    @pl.when((pl.program_id(0) == 0) & (step == 0))
    def _():
        for j in range(4):
            rows_ref[:, lax.rem(place[0] + j, 4)] = pieces[j][...]

    a = a_ref[...].reshape(4 * ROWS, 8 * ROWS)
    b = rows_ref[pl.ds(2 * step, 2)].reshape(8 * ROWS, FEW)
    term = jnp.dot(a, b, preferred_element_type=jnp.float32).reshape(out_ref.shape)

    @pl.when(step == 0)
    def _():
        out_ref[...] = term

    @pl.when(step > 0)
    def _():
        out_ref[...] += term


def product_few(factor, pieces):
    place = jnp.stack([lax.axis_index("y"), lax.axis_index("core")]).astype(jnp.int32)
    return pl.pallas_call(
        few_step,
        out_shape=[
            jax.ShapeDtypeStruct((2, 4, ROWS, FEW), jnp.float32),
            jax.ShapeDtypeStruct((8, 4, ROWS, FEW), jnp.bfloat16),
        ],
        grid_spec=pltpu.PrefetchScalarGridSpec(
            num_scalar_prefetch=1,
            grid=(2, 4),
            in_specs=[
                pl.BlockSpec((4, None, ROWS, 8 * ROWS), lambda h, q, place: (0, lax.rem(place[1] + 1 + h, 2), 0, q)),
            ] + [pl.BlockSpec((8, ROWS, FEW), lambda h, q, place: (0, 0, 0))] * 4,
            out_specs=[
                pl.BlockSpec((None, 4, ROWS, FEW), lambda h, q, place: (h, 0, 0, 0)),
                pl.BlockSpec((8, 4, ROWS, FEW), lambda h, q, place: (0, 0, 0, 0)),
            ],
        ),
        compiler_params=pltpu.CompilerParams(vmem_limit_bytes=16 * 1024 * 1024),
        cost_estimate=pl.CostEstimate(flops=2 * 8 * ROWS * M // 8 * FEW, bytes_accessed=8 * 1024 * 1024, transcendentals=0),
    )(place, factor.reshape(4, 2, ROWS, 32 * ROWS), *pieces)


def many_step(place, a_ref, b_ref, *refs):
    few_ref = rows_ref = None
    if len(refs) > 8:
        few_ref, theirs_ref, mine_ref, rows_ref = refs[:4]
    else:
        theirs_ref, mine_ref = refs[:2]
    a_held, b_held, total, a_sem, b_sem, rows_sem = refs[-6:]
    steps, deep = a_held.shape[0], a_held.shape[2]
    inward = [
        (
            pltpu.make_async_copy(a_ref.at[:, pl.ds(q * deep, deep)], a_held.at[q], a_sem.at[q]),
            pltpu.make_async_copy(b_ref.at[pl.ds(q * deep, deep)], b_held.at[q], b_sem.at[q]),
        )
        for q in range(steps)
    ]
    outward = []

    def start(copies):
        for copy in copies:
            copy.start()

    for q in range(steps):
        start(inward[q])
    if rows_ref is not None:
        outward.append(pltpu.make_async_copy(few_ref, rows_ref.at[:, pl.ds(0, FEW)], rows_sem.at[steps]))
        start(outward)
    for q in range(steps):
        for copy in inward[q]:
            copy.wait()
        if rows_ref is not None:
            outward.append(pltpu.make_async_copy(
                b_held.at[q], rows_ref.at[pl.ds(q * deep, deep), pl.ds(FEW, K - FEW)], rows_sem.at[q]))
            start(outward[-1:])
        term = jnp.dot(a_held[q], b_held[q], preferred_element_type=jnp.float32).reshape(total.shape)
        if q == 0:
            total[...] = term
        else:
            total[...] += term
    theirs_ref[...] = total[:, 1 - place[0]]
    mine_ref[...] = total[:, place[0]]
    for copy in outward:
        copy.wait()


def product_many(factor, many, place, few=None):
    steps = 7
    deep = 32 * ROWS // steps
    operands = [factor, many] if few is None else [factor, many, few]
    part = jax.ShapeDtypeStruct((4, ROWS, K - FEW), jnp.float32)
    return pl.pallas_call(
        many_step,
        out_shape=[part, part] + [jax.ShapeDtypeStruct((32 * ROWS, K), jnp.bfloat16)] * (len(operands) - 2),
        in_specs=[SMEM, HBM, HBM] + [VMEM] * (len(operands) - 2),
        out_specs=[VMEM, VMEM] + [HBM] * (len(operands) - 2),
        scratch_shapes=[
            pltpu.VMEM((steps, 8 * ROWS, deep), jnp.bfloat16),
            pltpu.VMEM((steps, deep, K - FEW), jnp.bfloat16),
            pltpu.VMEM((4, 2, ROWS, K - FEW), jnp.float32),
            pltpu.SemaphoreType.DMA((steps,)),
            pltpu.SemaphoreType.DMA((steps,)),
            pltpu.SemaphoreType.DMA((steps + 1,)),
        ],
        compiler_params=pltpu.CompilerParams(vmem_limit_bytes=60 * 1024 * 1024),
        cost_estimate=pl.CostEstimate(flops=2 * 8 * ROWS * M // 8 * (K - FEW), bytes_accessed=12 * 1024 * 1024, transcendentals=0),
    )(place, *operands)


def summed_product(factor, few, many, keep):
    place = core_place()
    many, pieces = gathered_rows(few, many)
    both, ordered = product_few(factor, pieces)
    few = both[1] + permute(both[0], other_core)
    many, few = lax.optimization_barrier((many, few))
    theirs, mine, *rest = product_many(factor, many, place, ordered.reshape(32 * ROWS, FEW) if keep else None)
    total = jnp.concatenate([few, mine + permute(theirs, other_core)], axis=2)
    return summed_gram(place, exchange(total, "x")), rest


def gram_inverse(packed, moved=None):
    share = packed[1] + permute(packed[0], other_core)
    share = jnp.sum(exchange(share.reshape(16, 5 * B // 16, B), ("y", "x")), axis=0)
    share, moved = lax.optimization_barrier((share, moved))
    share = jnp.sum(exchange(copies(share, "z"), "z"), axis=0)
    share = exchange(copies(share, ("y", "x")), ("y", "x")).reshape(5, B, B)
    return inverse_factor(core_place(), share, permute(share, other_core)), moved


def shards(factor, basis):
    scale = math.sqrt(M)
    rows = lax.dynamic_slice_in_dim(basis, lax.axis_index(("x", "core")) * ROWS, ROWS, 0)
    own = permute(rows, chunk_place)
    (first, packed), _ = summed_product(factor, own[:, :FEW], gather_y_small(own[:, FEW:]), False)
    inverse, moved = gram_inverse(packed, permute(first, chunk_place))
    middle = (dot(gather_y_small(moved), inverse, 1, 1) * scale).astype(jnp.bfloat16)
    own = lax.dynamic_slice_in_dim(middle, lax.axis_index("y") * ROWS, ROWS, 0)
    (second, packed), (column_basis,) = summed_product(factor, own[:, :FEW], middle[:, FEW:], True)
    inverse, _ = gram_inverse(packed)
    return dot(second, inverse, 1, 1) * scale, column_basis


def solution(mesh):
    fine = jax.sharding.Mesh(mesh.devices.reshape(SIZES), AXES)
    return jax.shard_map(
        shards,
        mesh=fine,
        in_specs=(P(("z", "y"), ("x", "core")), P(("z", "y"), None)),
        out_specs=(P(AXES, None), P(("x", "core"), None)),
        check_vma=False,
    )
```

```python
import math

import jax
import jax.numpy as jnp
from jax import lax
from jax.experimental import pallas as pl
from jax.experimental.pallas import tpu as pltpu
from jax.sharding import PartitionSpec as P

M = 28672
K = 512
B = 128
R = 8
AXES = ("z", "y", "x", "core")
SIZES = (8, 4, 4, 2)
HALF = K // 2
FEW = 128
ROWS = M // 256


def dot(a, b, ca, cb):
    return lax.dot_general(a, b, (((ca,), (cb,)), ((), ())), precision=lax.Precision.HIGHEST,
                           preferred_element_type=jnp.float32)


def reciprocal_rows(top, at, lane, sub):
    wide = [jnp.broadcast_to(top[:, at + j:at + j + 1], (R, B)) for j in range(R)]
    e = {(i, j): jnp.broadcast_to(wide[j][i:i + 1, :], (R, B)) for i in range(R) for j in range(i + 1)}
    inside = (lane >= at) & (lane < at + R)
    rhs = jnp.where(inside, jnp.where(lane - at == sub, 1.0, 0.0), top)
    row = [jnp.broadcast_to(rhs[i:i + 1, :], (R, B)) for i in range(R)]
    ratio, solved, final = {}, [None] * R, [None] * R
    for k in range(0, R, 2):
        a, b, c = e[k, k], e[k + 1, k], e[k + 1, k + 1]
        det = a * c - b * b
        over = 1.0 / det
        for i in range(k + 2, R):
            ratio[i, k] = (e[i, k] * c - e[i, k + 1] * b) * over
            ratio[i, k + 1] = (e[i, k + 1] * a - e[i, k] * b) * over
        for i in range(k + 2, R):
            for j in range(k + 2, i + 1):
                if i < k + 4:
                    one = (e[i, k] * c - e[i, k + 1] * b) * e[j, k]
                    two = (e[i, k + 1] * a - e[i, k] * b) * e[j, k + 1]
                    e[i, j] = e[i, j] - (one + two) * over
                else:
                    e[i, j] = e[i, j] - (ratio[i, k] * e[j, k] + ratio[i, k + 1] * e[j, k + 1])
            row[i] = row[i] - (ratio[i, k] * row[k] + ratio[i, k + 1] * row[k + 1])
        solved[k] = (c * row[k] - b * row[k + 1]) * over
        solved[k + 1] = (a * row[k + 1] - b * row[k]) * over
        root = lax.rsqrt(a)
        final[k] = row[k] * root
        final[k + 1] = (row[k + 1] - (b * root) * final[k]) * (lax.rsqrt(det) * (a * root))
    back = [None] * R
    for k in reversed(range(R)):
        z = solved[k]
        for i in reversed(range(k + 2 - k % 2, R)):
            z = z - ratio[i, k] * back[i]
        back[k] = z
    out = final[0]
    for k in range(1, R):
        out = jnp.where(sub == k, final[k], out)
    return jnp.where(lane < at + R, out, 0.0), back, inside


def leaf(block):
    n = B // R
    w = [block[R * i:R * i + R, :] for i in range(n)]
    lane = lax.broadcasted_iota(jnp.int32, (R, B), 1)
    sub = lax.broadcasted_iota(jnp.int32, (R, B), 0)
    done = []
    for p in range(n):
        at = R * p
        rows, back, inside = reciprocal_rows(w[p], at, lane, sub)
        done.append(rows)
        for i in range(p + 1, n):
            new = jnp.where(inside, 0.0, w[i])
            for j in reversed(range(R)):
                new = new - jnp.broadcast_to(w[i][:, at + j:at + j + 1], (R, B)) * back[j]
            w[i] = new
    return jnp.concatenate(done, axis=0)


def unit(n):
    return lax.broadcasted_iota(jnp.int32, (n, n), 0) == lax.broadcasted_iota(jnp.int32, (n, n), 1)


def halves():
    lower = [(i, j) for i in range(K // B) for j in range(i + 1)]
    return lower[:5], lower[5:]


def gram_step(place, parts_ref, sum_ref, packed_ref):
    total = (parts_ref[0] + parts_ref[1]) + (parts_ref[2] + parts_ref[3])
    sum_ref[...] = total
    for half, blocks in enumerate(halves()):
        slot = jnp.where(place[0] == half, 1, 0)
        for at, (i, j) in enumerate(blocks):
            packed_ref[slot, at] = dot(total[:, B * i:B * i + B], total[:, B * j:B * j + B], 0, 0)


def chol_inverse(place, own_ref, came_ref, out_ref, work):
    for half, blocks in enumerate(halves()):
        for at, (i, j) in enumerate(blocks):
            entry = jnp.where(place[0] == half, own_ref[at], came_ref[at])
            work[B * i:B * i + B, B * j:B * j + B] = entry
            if i != j:
                work[B * j:B * j + B, B * i:B * i + B] = entry.T
    gram = work[...]
    diagonal = jnp.where(unit(K), gram, 0.0)
    along = lax.rsqrt(jnp.sum(diagonal, axis=0, keepdims=True))
    work[...] = gram * along * lax.rsqrt(jnp.sum(diagonal, axis=1, keepdims=True))

    def block(b, _):
        at = pl.multiple_of(b * B, B)
        low = leaf(work[pl.ds(at, B), pl.ds(at, B)])
        work[pl.ds(at, B), pl.ds(at, B)] = jnp.where(unit(B), 1.0, 0.0)
        top = dot(low, work[pl.ds(at, B), :], 1, 0)
        lane = lax.broadcasted_iota(jnp.int32, (B, K), 1)
        out_ref[pl.ds(at, B), :] = jnp.where(lane < at + B, top, 0.0) * along
        for i in range(1, K // B):
            @pl.when(i > b)
            def _():
                to = B * i
                work[to:to + B, pl.ds(at, B)] = jnp.zeros((B, B), jnp.float32)
                work[to:to + B, :] = work[to:to + B, :] - dot(top[:, to:to + B], top, 0, 0)
        return 0

    lax.fori_loop(0, K // B, block, 0)


VMEM = pl.BlockSpec(memory_space=pltpu.VMEM)
SMEM = pl.BlockSpec(memory_space=pltpu.SMEM)
HBM = pl.BlockSpec(memory_space=pl.ANY)


def core_place():
    return lax.axis_index("core").astype(jnp.int32).reshape(1)


def summed_gram(place, parts):
    return pl.pallas_call(
        gram_step,
        out_shape=[
            jax.ShapeDtypeStruct((ROWS, K), jnp.float32),
            jax.ShapeDtypeStruct((2, 5, B, B), jnp.float32),
        ],
        in_specs=[SMEM, VMEM],
        out_specs=[VMEM, VMEM],
        compiler_params=pltpu.CompilerParams(vmem_limit_bytes=12 * 1024 * 1024),
        cost_estimate=pl.CostEstimate(flops=2 * ROWS * K * K, bytes_accessed=8 * K * K, transcendentals=0),
    )(place, parts)


def inverse_factor(place, own, came):
    return pl.pallas_call(
        chol_inverse,
        out_shape=jax.ShapeDtypeStruct((K, K), jnp.float32),
        in_specs=[SMEM, VMEM, VMEM],
        out_specs=VMEM,
        scratch_shapes=[pltpu.VMEM((K, K), jnp.float32)],
        compiler_params=pltpu.CompilerParams(vmem_limit_bytes=12 * 1024 * 1024),
        cost_estimate=pl.CostEstimate(flops=150 * K ** 3, bytes_accessed=8 * K * K, transcendentals=0),
    )(place, own, came)


def permute(values, where):
    places = [(z, y, x, c) for z in range(8) for y in range(4) for x in range(4) for c in range(2)]
    index = {place: i for i, place in enumerate(places)}
    return lax.ppermute(values, AXES, [(index[p], index[where(*p)]) for p in places])


def other_core(z, y, x, c):
    return z, y, x, 1 - c


def exchange(pieces, axes):
    return lax.all_to_all(pieces, axes, 0, 0, tiled=True)


def copies(values, axes):
    return jnp.broadcast_to(values[None], (lax.axis_size(axes),) + values.shape)


def up(z, y, x, c):
    return z, (y + 1) % 4, x, c


def down(z, y, x, c):
    return z, (y - 1) % 4, x, c


def gather_y(own):
    half = own.shape[0] // 2
    before, after = permute(own, up), permute(own, down)
    far = jnp.concatenate([permute(before[:half], up), permute(after[half:], down)], axis=0)
    return [own, after, far, before]


def small_pieces(own):
    far = permute(own, lambda z, y, x, c: (z, (y + 2) % 4, x, c))
    return [own, permute(own, down), far, permute(own, up)]


def in_order(pieces):
    rows, width = pieces[0].shape
    out = jnp.zeros((4 * rows, width), pieces[0].dtype)
    for step, piece in enumerate(pieces):
        out = lax.dynamic_update_slice_in_dim(out, piece, lax.rem(lax.axis_index("y") + step, 4) * rows, 0)
    return out


def chunk_place(z, y, x, c):
    chunk = 8 * y + 2 * x + c
    return chunk // 4, chunk % 4, z // 2, z % 2


def gathered_rows(few, many):
    many, few = lax.optimization_barrier((many, few))
    return lax.all_gather(many, "z", axis=0, tiled=True), gather_y(exchange(copies(few, "z"), "z"))


def few_step(place, a_ref, *refs):
    pieces, out_ref, rows_ref = refs[:4], refs[4], refs[5]
    step = pl.program_id(1)

    @pl.when((pl.program_id(0) == 0) & (step == 0))
    def _():
        for j in range(4):
            rows_ref[:, lax.rem(place[0] + j, 4)] = pieces[j][...]

    a = a_ref[...].reshape(4 * ROWS, 8 * ROWS)
    b = rows_ref[pl.ds(2 * step, 2)].reshape(8 * ROWS, FEW)
    term = jnp.dot(a, b, preferred_element_type=jnp.float32).reshape(out_ref.shape)

    @pl.when(step == 0)
    def _():
        out_ref[...] = term

    @pl.when(step > 0)
    def _():
        out_ref[...] += term


def product_few(factor, pieces):
    place = jnp.stack([lax.axis_index("y"), lax.axis_index("core")]).astype(jnp.int32)
    return pl.pallas_call(
        few_step,
        out_shape=[
            jax.ShapeDtypeStruct((2, 4, ROWS, FEW), jnp.float32),
            jax.ShapeDtypeStruct((8, 4, ROWS, FEW), jnp.bfloat16),
        ],
        grid_spec=pltpu.PrefetchScalarGridSpec(
            num_scalar_prefetch=1,
            grid=(2, 4),
            in_specs=[
                pl.BlockSpec((4, None, ROWS, 8 * ROWS), lambda h, q, place: (0, lax.rem(place[1] + 1 + h, 2), 0, q)),
            ] + [pl.BlockSpec((8, ROWS, FEW), lambda h, q, place: (0, 0, 0))] * 4,
            out_specs=[
                pl.BlockSpec((None, 4, ROWS, FEW), lambda h, q, place: (h, 0, 0, 0)),
                pl.BlockSpec((8, 4, ROWS, FEW), lambda h, q, place: (0, 0, 0, 0)),
            ],
        ),
        compiler_params=pltpu.CompilerParams(vmem_limit_bytes=16 * 1024 * 1024),
        cost_estimate=pl.CostEstimate(flops=2 * 8 * ROWS * M // 8 * FEW, bytes_accessed=8 * 1024 * 1024, transcendentals=0),
    )(place, factor.reshape(4, 2, ROWS, 32 * ROWS), *pieces)


def many_step(place, a_ref, b_ref, *refs):
    few_ref = rows_ref = None
    if len(refs) > 8:
        few_ref, theirs_ref, mine_ref, rows_ref = refs[:4]
    else:
        theirs_ref, mine_ref = refs[:2]
    a_held, b_held, total, a_sem, b_sem, rows_sem = refs[-6:]
    steps, deep = a_held.shape[0], a_held.shape[2]
    inward = [
        (
            pltpu.make_async_copy(a_ref.at[:, pl.ds(q * deep, deep)], a_held.at[q], a_sem.at[q]),
            pltpu.make_async_copy(b_ref.at[pl.ds(q * deep, deep)], b_held.at[q], b_sem.at[q]),
        )
        for q in range(steps)
    ]
    outward = []

    def start(copies):
        for copy in copies:
            copy.start()

    for q in range(steps):
        start(inward[q])
    if rows_ref is not None:
        outward.append(pltpu.make_async_copy(few_ref, rows_ref.at[:, pl.ds(0, FEW)], rows_sem.at[steps]))
        start(outward)
    for q in range(steps):
        for copy in inward[q]:
            copy.wait()
        if rows_ref is not None:
            outward.append(pltpu.make_async_copy(
                b_held.at[q], rows_ref.at[pl.ds(q * deep, deep), pl.ds(FEW, K - FEW)], rows_sem.at[q]))
            start(outward[-1:])
        term = jnp.dot(a_held[q], b_held[q], preferred_element_type=jnp.float32).reshape(total.shape)
        if q == 0:
            total[...] = term
        else:
            total[...] += term
    theirs_ref[...] = total[:, 1 - place[0]]
    mine_ref[...] = total[:, place[0]]
    for copy in outward:
        copy.wait()


def product_many(factor, many, place, few=None):
    steps = 7
    deep = 32 * ROWS // steps
    operands = [factor, many] if few is None else [factor, many, few]
    part = jax.ShapeDtypeStruct((4, ROWS, K - FEW), jnp.float32)
    return pl.pallas_call(
        many_step,
        out_shape=[part, part] + [jax.ShapeDtypeStruct((32 * ROWS, K), jnp.bfloat16)] * (len(operands) - 2),
        in_specs=[SMEM, HBM, HBM] + [VMEM] * (len(operands) - 2),
        out_specs=[VMEM, VMEM] + [HBM] * (len(operands) - 2),
        scratch_shapes=[
            pltpu.VMEM((steps, 8 * ROWS, deep), jnp.bfloat16),
            pltpu.VMEM((steps, deep, K - FEW), jnp.bfloat16),
            pltpu.VMEM((4, 2, ROWS, K - FEW), jnp.float32),
            pltpu.SemaphoreType.DMA((steps,)),
            pltpu.SemaphoreType.DMA((steps,)),
            pltpu.SemaphoreType.DMA((steps + 1,)),
        ],
        compiler_params=pltpu.CompilerParams(vmem_limit_bytes=60 * 1024 * 1024),
        cost_estimate=pl.CostEstimate(flops=2 * 8 * ROWS * M // 8 * (K - FEW), bytes_accessed=12 * 1024 * 1024, transcendentals=0),
    )(place, *operands)


def summed_product(factor, few, many, keep):
    place = core_place()
    many, pieces = gathered_rows(few, many)
    both, ordered = product_few(factor, pieces)
    few = both[1] + permute(both[0], other_core)
    many, few = lax.optimization_barrier((many, few))
    theirs, mine, *rest = product_many(factor, many, place, ordered.reshape(32 * ROWS, FEW) if keep else None)
    total = jnp.concatenate([few, mine + permute(theirs, other_core)], axis=2)
    return summed_gram(place, exchange(total, "x")), rest


def gram_inverse(packed, moved=None):
    share = packed[1] + permute(packed[0], other_core)
    share = jnp.sum(exchange(share.reshape(16, 5 * B // 16, B), ("y", "x")), axis=0)
    share = jnp.sum(exchange(copies(share, "z"), "z"), axis=0)
    share = exchange(copies(share, ("y", "x")), ("y", "x")).reshape(5, B, B)
    share, moved = lax.optimization_barrier((share, moved))
    return inverse_factor(core_place(), share, permute(share, other_core)), moved


def shards(factor, basis):
    scale = math.sqrt(M)
    rows = lax.dynamic_slice_in_dim(basis, lax.axis_index(("x", "core")) * ROWS, ROWS, 0)
    own = permute(rows, chunk_place)
    (first, packed), _ = summed_product(factor, own[:, :FEW], in_order(small_pieces(own[:, FEW:])), False)
    inverse, moved = gram_inverse(packed, permute(first, chunk_place))
    inverse, pieces = lax.optimization_barrier((inverse, small_pieces(moved)))
    middle = (dot(in_order(pieces), inverse, 1, 1) * scale).astype(jnp.bfloat16)
    own = lax.dynamic_slice_in_dim(middle, lax.axis_index("y") * ROWS, ROWS, 0)
    (second, packed), (column_basis,) = summed_product(factor, own[:, :FEW], middle[:, FEW:], True)
    inverse, _ = gram_inverse(packed)
    return dot(second, inverse, 1, 1) * scale, column_basis


def solution(mesh):
    fine = jax.sharding.Mesh(mesh.devices.reshape(SIZES), AXES)
    return jax.shard_map(
        shards,
        mesh=fine,
        in_specs=(P(("z", "y"), ("x", "core")), P(("z", "y"), None)),
        out_specs=(P(AXES, None), P(("x", "core"), None)),
        check_vma=False,
    )
```

```python
import math

import jax
import jax.numpy as jnp
from jax import lax
from jax.experimental import pallas as pl
from jax.experimental.pallas import tpu as pltpu
from jax.sharding import PartitionSpec as P

M = 28672
K = 512
B = 128
R = 8
AXES = ("z", "y", "x", "core")
SIZES = (8, 4, 4, 2)
HALF = K // 2
FEW = 128
ROWS = M // 256


def dot(a, b, ca, cb):
    return lax.dot_general(a, b, (((ca,), (cb,)), ((), ())), precision=lax.Precision.HIGHEST,
                           preferred_element_type=jnp.float32)


def reciprocal_rows(top, at, lane, sub):
    wide = [jnp.broadcast_to(top[:, at + j:at + j + 1], (R, B)) for j in range(R)]
    e = {(i, j): jnp.broadcast_to(wide[j][i:i + 1, :], (R, B)) for i in range(R) for j in range(i + 1)}
    inside = (lane >= at) & (lane < at + R)
    rhs = jnp.where(inside, jnp.where(lane - at == sub, 1.0, 0.0), top)
    row = [jnp.broadcast_to(rhs[i:i + 1, :], (R, B)) for i in range(R)]
    ratio, solved, final = {}, [None] * R, [None] * R
    for k in range(0, R, 2):
        a, b, c = e[k, k], e[k + 1, k], e[k + 1, k + 1]
        det = a * c - b * b
        over = 1.0 / det
        for i in range(k + 2, R):
            ratio[i, k] = (e[i, k] * c - e[i, k + 1] * b) * over
            ratio[i, k + 1] = (e[i, k + 1] * a - e[i, k] * b) * over
        for i in range(k + 2, R):
            for j in range(k + 2, i + 1):
                if i < k + 4:
                    one = (e[i, k] * c - e[i, k + 1] * b) * e[j, k]
                    two = (e[i, k + 1] * a - e[i, k] * b) * e[j, k + 1]
                    e[i, j] = e[i, j] - (one + two) * over
                else:
                    e[i, j] = e[i, j] - (ratio[i, k] * e[j, k] + ratio[i, k + 1] * e[j, k + 1])
            row[i] = row[i] - (ratio[i, k] * row[k] + ratio[i, k + 1] * row[k + 1])
        solved[k] = (c * row[k] - b * row[k + 1]) * over
        solved[k + 1] = (a * row[k + 1] - b * row[k]) * over
        root = lax.rsqrt(a)
        final[k] = row[k] * root
        final[k + 1] = (row[k + 1] - (b * root) * final[k]) * (lax.rsqrt(det) * (a * root))
    back = [None] * R
    for k in reversed(range(R)):
        z = solved[k]
        for i in reversed(range(k + 2 - k % 2, R)):
            z = z - ratio[i, k] * back[i]
        back[k] = z
    out = final[0]
    for k in range(1, R):
        out = jnp.where(sub == k, final[k], out)
    return jnp.where(lane < at + R, out, 0.0), back, inside


def leaf(block):
    n = B // R
    w = [block[R * i:R * i + R, :] for i in range(n)]
    lane = lax.broadcasted_iota(jnp.int32, (R, B), 1)
    sub = lax.broadcasted_iota(jnp.int32, (R, B), 0)
    done = []
    for p in range(n):
        at = R * p
        rows, back, inside = reciprocal_rows(w[p], at, lane, sub)
        done.append(rows)
        for i in range(p + 1, n):
            new = jnp.where(inside, 0.0, w[i])
            for j in reversed(range(R)):
                new = new - jnp.broadcast_to(w[i][:, at + j:at + j + 1], (R, B)) * back[j]
            w[i] = new
    return jnp.concatenate(done, axis=0)


def unit(n):
    return lax.broadcasted_iota(jnp.int32, (n, n), 0) == lax.broadcasted_iota(jnp.int32, (n, n), 1)


def halves():
    lower = [(i, j) for i in range(K // B) for j in range(i + 1)]
    return lower[:5], lower[5:]


def gram_step(place, parts_ref, sum_ref, packed_ref):
    total = (parts_ref[0] + parts_ref[1]) + (parts_ref[2] + parts_ref[3])
    sum_ref[...] = total
    for half, blocks in enumerate(halves()):
        slot = jnp.where(place[0] == half, 1, 0)
        for at, (i, j) in enumerate(blocks):
            packed_ref[slot, at] = dot(total[:, B * i:B * i + B], total[:, B * j:B * j + B], 0, 0)


def chol_inverse(place, own_ref, came_ref, out_ref, work):
    for half, blocks in enumerate(halves()):
        for at, (i, j) in enumerate(blocks):
            entry = jnp.where(place[0] == half, own_ref[at], came_ref[at])
            work[B * i:B * i + B, B * j:B * j + B] = entry
            if i != j:
                work[B * j:B * j + B, B * i:B * i + B] = entry.T
    gram = work[...]
    diagonal = jnp.where(unit(K), gram, 0.0)
    along = lax.rsqrt(jnp.sum(diagonal, axis=0, keepdims=True))
    work[...] = gram * along * lax.rsqrt(jnp.sum(diagonal, axis=1, keepdims=True))

    def block(b, _):
        at = pl.multiple_of(b * B, B)
        low = leaf(work[pl.ds(at, B), pl.ds(at, B)])
        work[pl.ds(at, B), pl.ds(at, B)] = jnp.where(unit(B), 1.0, 0.0)
        top = dot(low, work[pl.ds(at, B), :], 1, 0)
        lane = lax.broadcasted_iota(jnp.int32, (B, K), 1)
        out_ref[pl.ds(at, B), :] = jnp.where(lane < at + B, top, 0.0) * along
        for last in range(K // B - 1):
            @pl.when(b == last)
            def _():
                to = B * (last + 1)
                work[to:, B * last:to] = jnp.zeros((K - to, B), jnp.float32)
                work[to:, :] = work[to:, :] - dot(top[:, to:], top, 0, 0)
        return 0

    lax.fori_loop(0, K // B, block, 0)


VMEM = pl.BlockSpec(memory_space=pltpu.VMEM)
SMEM = pl.BlockSpec(memory_space=pltpu.SMEM)
HBM = pl.BlockSpec(memory_space=pl.ANY)


def core_place():
    return lax.axis_index("core").astype(jnp.int32).reshape(1)


def summed_gram(place, parts):
    return pl.pallas_call(
        gram_step,
        out_shape=[
            jax.ShapeDtypeStruct((ROWS, K), jnp.float32),
            jax.ShapeDtypeStruct((2, 5, B, B), jnp.float32),
        ],
        in_specs=[SMEM, VMEM],
        out_specs=[VMEM, VMEM],
        compiler_params=pltpu.CompilerParams(vmem_limit_bytes=12 * 1024 * 1024),
        cost_estimate=pl.CostEstimate(flops=2 * ROWS * K * K, bytes_accessed=8 * K * K, transcendentals=0),
    )(place, parts)


def inverse_factor(place, own, came):
    return pl.pallas_call(
        chol_inverse,
        out_shape=jax.ShapeDtypeStruct((K, K), jnp.float32),
        in_specs=[SMEM, VMEM, VMEM],
        out_specs=VMEM,
        scratch_shapes=[pltpu.VMEM((K, K), jnp.float32)],
        compiler_params=pltpu.CompilerParams(vmem_limit_bytes=12 * 1024 * 1024),
        cost_estimate=pl.CostEstimate(flops=150 * K ** 3, bytes_accessed=8 * K * K, transcendentals=0),
    )(place, own, came)


def permute(values, where):
    places = [(z, y, x, c) for z in range(8) for y in range(4) for x in range(4) for c in range(2)]
    index = {place: i for i, place in enumerate(places)}
    return lax.ppermute(values, AXES, [(index[p], index[where(*p)]) for p in places])


def other_core(z, y, x, c):
    return z, y, x, 1 - c


def exchange(pieces, axes):
    return lax.all_to_all(pieces, axes, 0, 0, tiled=True)


def copies(values, axes):
    return jnp.broadcast_to(values[None], (lax.axis_size(axes),) + values.shape)


def up(z, y, x, c):
    return z, (y + 1) % 4, x, c


def down(z, y, x, c):
    return z, (y - 1) % 4, x, c


def gather_y(own):
    half = own.shape[0] // 2
    before, after = permute(own, up), permute(own, down)
    far = jnp.concatenate([permute(before[:half], up), permute(after[half:], down)], axis=0)
    return [own, after, far, before]


def small_pieces(own):
    far = permute(own, lambda z, y, x, c: (z, (y + 2) % 4, x, c))
    return [own, permute(own, down), far, permute(own, up)]


def in_order(pieces):
    rows, width = pieces[0].shape
    out = jnp.zeros((4 * rows, width), pieces[0].dtype)
    for step, piece in enumerate(pieces):
        out = lax.dynamic_update_slice_in_dim(out, piece, lax.rem(lax.axis_index("y") + step, 4) * rows, 0)
    return out


def column_place(z, y, x, c):
    return 2 * x + c, y, z // 2, z % 2


def gathered_rows(own):
    many, few = lax.optimization_barrier((in_order(small_pieces(own[:, FEW:])), own[:, :FEW]))
    many = lax.all_gather(many, "z", axis=0, tiled=True).reshape(8, 4, ROWS, K - FEW)
    return many, gather_y(exchange(copies(few, "z"), "z"))


def few_step(place, a_ref, *refs):
    pieces, out_ref, rows_ref = refs[:4], refs[4], refs[5]
    step = pl.program_id(1)

    @pl.when((pl.program_id(0) == 0) & (step == 0))
    def _():
        for j in range(4):
            rows_ref[lax.rem(place[0] + j, 4)] = pieces[j][...]

    a = a_ref[...].reshape(4 * ROWS, 8 * ROWS)
    b = rows_ref[step].reshape(8 * ROWS, FEW)
    term = jnp.dot(a, b, preferred_element_type=jnp.float32).reshape(out_ref.shape)

    @pl.when(step == 0)
    def _():
        out_ref[...] = term

    @pl.when(step > 0)
    def _():
        out_ref[...] += term


def product_few(factor, pieces):
    place = jnp.stack([lax.axis_index("y"), lax.axis_index("core")]).astype(jnp.int32)
    return pl.pallas_call(
        few_step,
        out_shape=[
            jax.ShapeDtypeStruct((2, 4, ROWS, FEW), jnp.float32),
            jax.ShapeDtypeStruct((4, 8, ROWS, FEW), jnp.bfloat16),
        ],
        grid_spec=pltpu.PrefetchScalarGridSpec(
            num_scalar_prefetch=1,
            grid=(2, 4),
            in_specs=[
                pl.BlockSpec((4, None, ROWS, 8 * ROWS), lambda h, q, place: (0, lax.rem(place[1] + 1 + h, 2), 0, q)),
            ] + [pl.BlockSpec((8, ROWS, FEW), lambda h, q, place: (0, 0, 0))] * 4,
            out_specs=[
                pl.BlockSpec((None, 4, ROWS, FEW), lambda h, q, place: (h, 0, 0, 0)),
                pl.BlockSpec((4, 8, ROWS, FEW), lambda h, q, place: (0, 0, 0, 0)),
            ],
        ),
        compiler_params=pltpu.CompilerParams(vmem_limit_bytes=16 * 1024 * 1024),
        cost_estimate=pl.CostEstimate(flops=2 * 8 * ROWS * M // 8 * FEW, bytes_accessed=8 * 1024 * 1024, transcendentals=0),
    )(place, factor.reshape(4, 2, ROWS, 32 * ROWS), *pieces)


def many_step(place, a_ref, b_ref, *refs):
    few_ref = rows_ref = None
    if len(refs) > 8:
        few_ref, theirs_ref, mine_ref, rows_ref = refs[:4]
    else:
        theirs_ref, mine_ref = refs[:2]
    a_held, b_held, total, a_sem, b_sem, rows_sem = refs[-6:]
    steps, deep = 4, 8 * ROWS
    inward = [
        (
            pltpu.make_async_copy(a_ref.at[:, pl.ds(q * deep, deep)], a_held.at[q], a_sem.at[q]),
            pltpu.make_async_copy(b_ref.at[:, q], b_held.at[q], b_sem.at[q]),
        )
        for q in range(steps)
    ]
    outward = []

    def start(copies):
        for copy in copies:
            copy.start()

    for q in range(steps):
        start(inward[q])
    if rows_ref is not None:
        outward.append(pltpu.make_async_copy(few_ref, rows_ref.at[:, :, :, pl.ds(0, FEW)], rows_sem.at[steps]))
        start(outward)
    for q in range(steps):
        for copy in inward[q]:
            copy.wait()
        if rows_ref is not None:
            outward.append(pltpu.make_async_copy(
                b_held.at[q], rows_ref.at[q, :, :, pl.ds(FEW, K - FEW)], rows_sem.at[q]))
            start(outward[-1:])
        b = b_held[q].reshape(deep, K - FEW)
        term = jnp.dot(a_held[q], b, preferred_element_type=jnp.float32).reshape(total.shape)
        if q == 0:
            total[...] = term
        else:
            total[...] += term
    theirs_ref[...] = total[:, 1 - place[0]]
    mine_ref[...] = total[:, place[0]]
    for copy in outward:
        copy.wait()


def product_many(factor, many, place, few=None):
    steps = 4
    operands = [factor, many] if few is None else [factor, many, few]
    part = jax.ShapeDtypeStruct((4, ROWS, K - FEW), jnp.float32)
    return pl.pallas_call(
        many_step,
        out_shape=[part, part] + [jax.ShapeDtypeStruct((4, 8, ROWS, K), jnp.bfloat16)] * (len(operands) - 2),
        in_specs=[SMEM, HBM, HBM] + [VMEM] * (len(operands) - 2),
        out_specs=[VMEM, VMEM] + [HBM] * (len(operands) - 2),
        scratch_shapes=[
            pltpu.VMEM((steps, 8 * ROWS, 8 * ROWS), jnp.bfloat16),
            pltpu.VMEM((steps, 8, ROWS, K - FEW), jnp.bfloat16),
            pltpu.VMEM((4, 2, ROWS, K - FEW), jnp.float32),
            pltpu.SemaphoreType.DMA((steps,)),
            pltpu.SemaphoreType.DMA((steps,)),
            pltpu.SemaphoreType.DMA((steps + 1,)),
        ],
        compiler_params=pltpu.CompilerParams(vmem_limit_bytes=60 * 1024 * 1024),
        cost_estimate=pl.CostEstimate(flops=2 * 8 * ROWS * M // 8 * (K - FEW), bytes_accessed=12 * 1024 * 1024, transcendentals=0),
    )(place, *operands)


def summed_product(factor, own, keep):
    place = core_place()
    many, pieces = gathered_rows(own)
    both, ordered = product_few(factor, pieces)
    few = both[1] + permute(both[0], other_core)
    many, few = lax.optimization_barrier((many, few))
    theirs, mine, *rest = product_many(factor, many, place, ordered if keep else None)
    total = jnp.concatenate([few, mine + permute(theirs, other_core)], axis=2)
    return summed_gram(place, exchange(total, "x")), rest


def gram_inverse(packed):
    share = packed[1] + permute(packed[0], other_core)
    share = jnp.sum(exchange(share.reshape(16, 5 * B // 16, B), ("y", "x")), axis=0)
    share = jnp.sum(exchange(copies(share, "z"), "z"), axis=0)
    share = exchange(copies(share, ("y", "x")), ("y", "x")).reshape(5, B, B)
    return inverse_factor(core_place(), share, permute(share, other_core))


def shards(factor, basis):
    scale = math.sqrt(M)
    rows = lax.dynamic_slice_in_dim(basis, lax.axis_index(("x", "core")) * ROWS, ROWS, 0)
    (first, packed), _ = summed_product(factor, permute(rows, column_place), False)
    inverse, moved = lax.optimization_barrier((gram_inverse(packed), permute(first, column_place)))
    middle = (dot(moved, inverse, 1, 1) * scale).astype(jnp.bfloat16)
    (second, packed), (column_basis,) = summed_product(factor, middle, True)
    return dot(second, gram_inverse(packed), 1, 1) * scale, column_basis.reshape(32 * ROWS, K)


def solution(mesh):
    fine = jax.sharding.Mesh(mesh.devices.reshape(SIZES), AXES)
    return jax.shard_map(
        shards,
        mesh=fine,
        in_specs=(P(("z", "y"), ("x", "core")), P(("z", "y"), None)),
        out_specs=(P(AXES, None), P(("x", "core"), None)),
        check_vma=False,
    )
```

```python
import math

import jax
import jax.numpy as jnp
from jax import lax
from jax.experimental import pallas as pl
from jax.experimental.pallas import tpu as pltpu
from jax.sharding import PartitionSpec as P

M = 28672
K = 512
B = 128
R = 8
AXES = ("z", "y", "x", "core")
SIZES = (8, 4, 4, 2)
HALF = K // 2
FEW = 128
ROWS = M // 256


def dot(a, b, ca, cb):
    return lax.dot_general(a, b, (((ca,), (cb,)), ((), ())), precision=lax.Precision.HIGHEST,
                           preferred_element_type=jnp.float32)


def eliminate(top, below, held, at, lane, sub):
    wide = [jnp.broadcast_to(top[:, at + j:at + j + 1], (R, B)) for j in range(R)]
    for j in range(R):
        held[j] = wide[j]
    e = {(i, j): jnp.broadcast_to(held[j, i:i + 1, :], (R, B)) for i in range(R) for j in range(i + 1)}
    inside = (lane >= at) & (lane < at + R)
    rhs = jnp.where(inside, jnp.where(lane - at == sub, 1.0, 0.0), top)
    row = [jnp.broadcast_to(rhs[i:i + 1, :], (R, B)) for i in range(R)]
    ratio, solved, final = {}, [None] * R, [None] * R
    side = [jnp.broadcast_to(below[:, at + j:at + j + 1], (R, B)) for j in range(R)]
    below = jnp.where(inside, 0.0, below)
    for k in range(0, R, 2):
        a, b, c = e[k, k], e[k + 1, k], e[k + 1, k + 1]
        det = a * c - b * b
        over = 1.0 / det
        for i in range(k + 2, R):
            ratio[i, k] = (e[i, k] * c - e[i, k + 1] * b) * over
            ratio[i, k + 1] = (e[i, k + 1] * a - e[i, k] * b) * over
        for i in range(k + 2, R):
            for j in range(k + 2, i + 1):
                if i < k + 4:
                    one = (e[i, k] * c - e[i, k + 1] * b) * e[j, k]
                    two = (e[i, k + 1] * a - e[i, k] * b) * e[j, k + 1]
                    e[i, j] = e[i, j] - (one + two) * over
                else:
                    e[i, j] = e[i, j] - (ratio[i, k] * e[j, k] + ratio[i, k + 1] * e[j, k + 1])
            row[i] = row[i] - (ratio[i, k] * row[k] + ratio[i, k + 1] * row[k + 1])
        one = (side[k] * c - side[k + 1] * b) * over
        two = (side[k + 1] * a - side[k] * b) * over
        for j in range(k + 2, R):
            side[j] = side[j] - (one * e[j, k] + two * e[j, k + 1])
        below = below - (one * row[k] + two * row[k + 1])
        solved[k] = (c * row[k] - b * row[k + 1]) * over
        solved[k + 1] = (a * row[k + 1] - b * row[k]) * over
        root = lax.rsqrt(a)
        final[k] = row[k] * root
        final[k + 1] = (row[k + 1] - (b * root) * final[k]) * (lax.rsqrt(det) * (a * root))
    back = [None] * R
    for k in reversed(range(R)):
        z = solved[k]
        for i in reversed(range(k + 2 - k % 2, R)):
            z = z - ratio[i, k] * back[i]
        back[k] = z
    out = final[0]
    for k in range(1, R):
        out = jnp.where(sub == k, final[k], out)
    return jnp.where(lane < at + R, out, 0.0), below, back, inside


def leaf(block, held):
    n = B // R
    w = [block[R * i:R * i + R, :] for i in range(n)]
    lane = lax.broadcasted_iota(jnp.int32, (R, B), 1)
    sub = lax.broadcasted_iota(jnp.int32, (R, B), 0)
    done = []
    for p in range(n):
        at = R * p
        last = p + 1 == n
        rows, below, back, inside = eliminate(w[p], w[p] if last else w[p + 1], held.at[p % 2], at, lane, sub)
        done.append(rows)
        if not last:
            w[p + 1] = below
        for i in range(p + 2, n):
            new = jnp.where(inside, 0.0, w[i])
            for j in reversed(range(R)):
                new = new - jnp.broadcast_to(w[i][:, at + j:at + j + 1], (R, B)) * back[j]
            w[i] = new
    return jnp.concatenate(done, axis=0)


def unit(n):
    return lax.broadcasted_iota(jnp.int32, (n, n), 0) == lax.broadcasted_iota(jnp.int32, (n, n), 1)


def halves():
    lower = [(i, j) for i in range(K // B) for j in range(i + 1)]
    return lower[:5], lower[5:]


def gram_step(place, parts_ref, sum_ref, packed_ref):
    total = (parts_ref[0] + parts_ref[1]) + (parts_ref[2] + parts_ref[3])
    sum_ref[...] = total
    for half, blocks in enumerate(halves()):
        slot = jnp.where(place[0] == half, 1, 0)
        for at, (i, j) in enumerate(blocks):
            packed_ref[slot, at] = dot(total[:, B * i:B * i + B], total[:, B * j:B * j + B], 0, 0)


def chol_inverse(place, own_ref, came_ref, out_ref, work, held):
    for half, blocks in enumerate(halves()):
        for at, (i, j) in enumerate(blocks):
            entry = jnp.where(place[0] == half, own_ref[at], came_ref[at])
            work[B * i:B * i + B, B * j:B * j + B] = entry
            if i != j:
                work[B * j:B * j + B, B * i:B * i + B] = entry.T
    gram = work[...]
    diagonal = jnp.where(unit(K), gram, 0.0)
    along = lax.rsqrt(jnp.sum(diagonal, axis=0, keepdims=True))
    work[...] = gram * along * lax.rsqrt(jnp.sum(diagonal, axis=1, keepdims=True))

    def block(b, _):
        at = pl.multiple_of(b * B, B)
        low = leaf(work[pl.ds(at, B), pl.ds(at, B)], held)
        work[pl.ds(at, B), pl.ds(at, B)] = jnp.where(unit(B), 1.0, 0.0)
        top = dot(low, work[pl.ds(at, B), :], 1, 0)
        lane = lax.broadcasted_iota(jnp.int32, (B, K), 1)
        out_ref[pl.ds(at, B), :] = jnp.where(lane < at + B, top, 0.0) * along
        for last in range(K // B - 1):
            @pl.when(b == last)
            def _():
                to = B * (last + 1)
                work[to:, B * last:to] = jnp.zeros((K - to, B), jnp.float32)
                work[to:, :] = work[to:, :] - dot(top[:, to:], top, 0, 0)
        return 0

    lax.fori_loop(0, K // B, block, 0)


VMEM = pl.BlockSpec(memory_space=pltpu.VMEM)
SMEM = pl.BlockSpec(memory_space=pltpu.SMEM)
HBM = pl.BlockSpec(memory_space=pl.ANY)


def core_place():
    return lax.axis_index("core").astype(jnp.int32).reshape(1)


def summed_gram(place, parts):
    return pl.pallas_call(
        gram_step,
        out_shape=[
            jax.ShapeDtypeStruct((ROWS, K), jnp.float32),
            jax.ShapeDtypeStruct((2, 5, B, B), jnp.float32),
        ],
        in_specs=[SMEM, VMEM],
        out_specs=[VMEM, VMEM],
        compiler_params=pltpu.CompilerParams(vmem_limit_bytes=12 * 1024 * 1024),
        cost_estimate=pl.CostEstimate(flops=2 * ROWS * K * K, bytes_accessed=8 * K * K, transcendentals=0),
    )(place, parts)


def inverse_factor(place, own, came):
    return pl.pallas_call(
        chol_inverse,
        out_shape=jax.ShapeDtypeStruct((K, K), jnp.float32),
        in_specs=[SMEM, VMEM, VMEM],
        out_specs=VMEM,
        scratch_shapes=[pltpu.VMEM((K, K), jnp.float32), pltpu.VMEM((2, R, R, B), jnp.float32)],
        compiler_params=pltpu.CompilerParams(vmem_limit_bytes=12 * 1024 * 1024),
        cost_estimate=pl.CostEstimate(flops=150 * K ** 3, bytes_accessed=8 * K * K, transcendentals=0),
    )(place, own, came)


def permute(values, where):
    places = [(z, y, x, c) for z in range(8) for y in range(4) for x in range(4) for c in range(2)]
    index = {place: i for i, place in enumerate(places)}
    return lax.ppermute(values, AXES, [(index[p], index[where(*p)]) for p in places])


def other_core(z, y, x, c):
    return z, y, x, 1 - c


def exchange(pieces, axes):
    return lax.all_to_all(pieces, axes, 0, 0, tiled=True)


def copies(values, axes):
    return jnp.broadcast_to(values[None], (lax.axis_size(axes),) + values.shape)


def up(z, y, x, c):
    return z, (y + 1) % 4, x, c


def down(z, y, x, c):
    return z, (y - 1) % 4, x, c


def gather_y(own):
    half = own.shape[0] // 2
    before, after = permute(own, up), permute(own, down)
    far = jnp.concatenate([permute(before[:half], up), permute(after[half:], down)], axis=0)
    return [own, after, far, before]


def small_pieces(own):
    far = permute(own, lambda z, y, x, c: (z, (y + 2) % 4, x, c))
    return [own, permute(own, down), far, permute(own, up)]


def in_order(pieces):
    rows, width = pieces[0].shape
    out = jnp.zeros((4 * rows, width), pieces[0].dtype)
    for step, piece in enumerate(pieces):
        out = lax.dynamic_update_slice_in_dim(out, piece, lax.rem(lax.axis_index("y") + step, 4) * rows, 0)
    return out


def column_place(z, y, x, c):
    return 2 * x + c, y, z // 2, z % 2


def gathered_rows(own):
    many, few = lax.optimization_barrier((in_order(small_pieces(own[:, FEW:])), own[:, :FEW]))
    many = lax.all_gather(many, "z", axis=0, tiled=True).reshape(8, 4, ROWS, K - FEW)
    return many, gather_y(exchange(copies(few, "z"), "z"))


def few_step(place, a_ref, *refs):
    pieces, out_ref, rows_ref = refs[:4], refs[4], refs[5]
    step = pl.program_id(1)

    @pl.when((pl.program_id(0) == 0) & (step == 0))
    def _():
        for j in range(4):
            rows_ref[lax.rem(place[0] + j, 4)] = pieces[j][...]

    a = a_ref[...].reshape(4 * ROWS, 8 * ROWS)
    b = rows_ref[step].reshape(8 * ROWS, FEW)
    term = jnp.dot(a, b, preferred_element_type=jnp.float32).reshape(out_ref.shape)

    @pl.when(step == 0)
    def _():
        out_ref[...] = term

    @pl.when(step > 0)
    def _():
        out_ref[...] += term


def product_few(factor, pieces):
    place = jnp.stack([lax.axis_index("y"), lax.axis_index("core")]).astype(jnp.int32)
    return pl.pallas_call(
        few_step,
        out_shape=[
            jax.ShapeDtypeStruct((2, 4, ROWS, FEW), jnp.float32),
            jax.ShapeDtypeStruct((4, 8, ROWS, FEW), jnp.bfloat16),
        ],
        grid_spec=pltpu.PrefetchScalarGridSpec(
            num_scalar_prefetch=1,
            grid=(2, 4),
            in_specs=[
                pl.BlockSpec((4, None, ROWS, 8 * ROWS), lambda h, q, place: (0, lax.rem(place[1] + 1 + h, 2), 0, q)),
            ] + [pl.BlockSpec((8, ROWS, FEW), lambda h, q, place: (0, 0, 0))] * 4,
            out_specs=[
                pl.BlockSpec((None, 4, ROWS, FEW), lambda h, q, place: (h, 0, 0, 0)),
                pl.BlockSpec((4, 8, ROWS, FEW), lambda h, q, place: (0, 0, 0, 0)),
            ],
        ),
        compiler_params=pltpu.CompilerParams(vmem_limit_bytes=16 * 1024 * 1024),
        cost_estimate=pl.CostEstimate(flops=2 * 8 * ROWS * M // 8 * FEW, bytes_accessed=8 * 1024 * 1024, transcendentals=0),
    )(place, factor.reshape(4, 2, ROWS, 32 * ROWS), *pieces)


def many_step(place, a_ref, b_ref, *refs):
    few_ref = rows_ref = None
    if len(refs) > 8:
        few_ref, theirs_ref, mine_ref, rows_ref = refs[:4]
    else:
        theirs_ref, mine_ref = refs[:2]
    a_held, b_held, total, a_sem, b_sem, rows_sem = refs[-6:]
    steps, deep = 4, 8 * ROWS
    inward = [
        (
            pltpu.make_async_copy(a_ref.at[:, pl.ds(q * deep, deep)], a_held.at[q], a_sem.at[q]),
            pltpu.make_async_copy(b_ref.at[:, q], b_held.at[q], b_sem.at[q]),
        )
        for q in range(steps)
    ]
    outward = []

    def start(copies):
        for copy in copies:
            copy.start()

    for q in range(steps):
        start(inward[q])
    if rows_ref is not None:
        outward.append(pltpu.make_async_copy(few_ref, rows_ref.at[:, :, :, pl.ds(0, FEW)], rows_sem.at[steps]))
        start(outward)
    for q in range(steps):
        for copy in inward[q]:
            copy.wait()
        if rows_ref is not None:
            outward.append(pltpu.make_async_copy(
                b_held.at[q], rows_ref.at[q, :, :, pl.ds(FEW, K - FEW)], rows_sem.at[q]))
            start(outward[-1:])
        b = b_held[q].reshape(deep, K - FEW)
        term = jnp.dot(a_held[q], b, preferred_element_type=jnp.float32).reshape(total.shape)
        if q == 0:
            total[...] = term
        else:
            total[...] += term
    theirs_ref[...] = total[:, 1 - place[0]]
    mine_ref[...] = total[:, place[0]]
    for copy in outward:
        copy.wait()


def product_many(factor, many, place, few=None):
    steps = 4
    operands = [factor, many] if few is None else [factor, many, few]
    part = jax.ShapeDtypeStruct((4, ROWS, K - FEW), jnp.float32)
    return pl.pallas_call(
        many_step,
        out_shape=[part, part] + [jax.ShapeDtypeStruct((4, 8, ROWS, K), jnp.bfloat16)] * (len(operands) - 2),
        in_specs=[SMEM, HBM, HBM] + [VMEM] * (len(operands) - 2),
        out_specs=[VMEM, VMEM] + [HBM] * (len(operands) - 2),
        scratch_shapes=[
            pltpu.VMEM((steps, 8 * ROWS, 8 * ROWS), jnp.bfloat16),
            pltpu.VMEM((steps, 8, ROWS, K - FEW), jnp.bfloat16),
            pltpu.VMEM((4, 2, ROWS, K - FEW), jnp.float32),
            pltpu.SemaphoreType.DMA((steps,)),
            pltpu.SemaphoreType.DMA((steps,)),
            pltpu.SemaphoreType.DMA((steps + 1,)),
        ],
        compiler_params=pltpu.CompilerParams(vmem_limit_bytes=60 * 1024 * 1024),
        cost_estimate=pl.CostEstimate(flops=2 * 8 * ROWS * M // 8 * (K - FEW), bytes_accessed=12 * 1024 * 1024, transcendentals=0),
    )(place, *operands)


def summed_product(factor, own, keep):
    place = core_place()
    many, pieces = gathered_rows(own)
    both, ordered = product_few(factor, pieces)
    few = both[1] + permute(both[0], other_core)
    many, few = lax.optimization_barrier((many, few))
    theirs, mine, *rest = product_many(factor, many, place, ordered if keep else None)
    total = jnp.concatenate([few, mine + permute(theirs, other_core)], axis=2)
    return summed_gram(place, exchange(total, "x")), rest


def gram_inverse(packed):
    share = packed[1] + permute(packed[0], other_core)
    share = jnp.sum(exchange(share.reshape(16, 5 * B // 16, B), ("y", "x")), axis=0)
    share = jnp.sum(exchange(copies(share, "z"), "z"), axis=0)
    share = exchange(copies(share, ("y", "x")), ("y", "x")).reshape(5, B, B)
    return inverse_factor(core_place(), share, permute(share, other_core))


def shards(factor, basis):
    scale = math.sqrt(M)
    rows = lax.dynamic_slice_in_dim(basis, lax.axis_index(("x", "core")) * ROWS, ROWS, 0)
    (first, packed), _ = summed_product(factor, permute(rows, column_place), False)
    inverse, moved = lax.optimization_barrier((gram_inverse(packed), permute(first, column_place)))
    middle = (dot(moved, inverse, 1, 1) * scale).astype(jnp.bfloat16)
    (second, packed), (column_basis,) = summed_product(factor, middle, True)
    return dot(second, gram_inverse(packed), 1, 1) * scale, column_basis.reshape(32 * ROWS, K)


def solution(mesh):
    fine = jax.sharding.Mesh(mesh.devices.reshape(SIZES), AXES)
    return jax.shard_map(
        shards,
        mesh=fine,
        in_specs=(P(("z", "y"), ("x", "core")), P(("z", "y"), None)),
        out_specs=(P(AXES, None), P(("x", "core"), None)),
        check_vma=False,
    )
```

```python
import math

import jax
import jax.numpy as jnp
from jax import lax
from jax.experimental import pallas as pl
from jax.experimental.pallas import tpu as pltpu
from jax.sharding import PartitionSpec as P

M = 28672
K = 512
B = 128
R = 8
AXES = ("z", "y", "x", "core")
SIZES = (8, 4, 4, 2)
HALF = K // 2
FEW = 128
ROWS = M // 256


def dot(a, b, ca, cb):
    return lax.dot_general(a, b, (((ca,), (cb,)), ((), ())), precision=lax.Precision.HIGHEST,
                           preferred_element_type=jnp.float32)


def eliminate(top, below, held, at, lane, sub):
    wide = [jnp.broadcast_to(top[:, at + j:at + j + 1], (R, B)) for j in range(R)]
    for j in range(R):
        held[j] = wide[j]
    e = {(i, j): jnp.broadcast_to(held[j, i:i + 1, :], (R, B)) for i in range(R) for j in range(i + 1)}
    inside = (lane >= at) & (lane < at + R)
    rhs = jnp.where(inside, jnp.where(lane - at == sub, 1.0, 0.0), top)
    row = [jnp.broadcast_to(rhs[i:i + 1, :], (R, B)) for i in range(R)]
    ratio, solved, final = {}, [None] * R, [None] * R
    side = [jnp.broadcast_to(below[:, at + j:at + j + 1], (R, B)) for j in range(R)]
    below = jnp.where(inside, 0.0, below)
    for k in range(0, R, 2):
        a, b, c = e[k, k], e[k + 1, k], e[k + 1, k + 1]
        det = a * c - b * b
        over = 1.0 / det
        for i in range(k + 2, R):
            ratio[i, k] = (e[i, k] * c - e[i, k + 1] * b) * over
            ratio[i, k + 1] = (e[i, k + 1] * a - e[i, k] * b) * over
        for i in range(k + 2, R):
            for j in range(k + 2, i + 1):
                if i < k + 4:
                    one = (e[i, k] * c - e[i, k + 1] * b) * e[j, k]
                    two = (e[i, k + 1] * a - e[i, k] * b) * e[j, k + 1]
                    e[i, j] = e[i, j] - (one + two) * over
                else:
                    e[i, j] = e[i, j] - (ratio[i, k] * e[j, k] + ratio[i, k + 1] * e[j, k + 1])
            row[i] = row[i] - (ratio[i, k] * row[k] + ratio[i, k + 1] * row[k + 1])
        one = (side[k] * c - side[k + 1] * b) * over
        two = (side[k + 1] * a - side[k] * b) * over
        for j in range(k + 2, R):
            side[j] = side[j] - (one * e[j, k] + two * e[j, k + 1])
        below = below - (one * row[k] + two * row[k + 1])
        solved[k] = (c * row[k] - b * row[k + 1]) * over
        solved[k + 1] = (a * row[k + 1] - b * row[k]) * over
        root = lax.rsqrt(a)
        final[k] = row[k] * root
        final[k + 1] = (row[k + 1] - (b * root) * final[k]) * (lax.rsqrt(det) * (a * root))
    back = [None] * R
    for k in reversed(range(R)):
        z = solved[k]
        for i in reversed(range(k + 2 - k % 2, R)):
            z = z - ratio[i, k] * back[i]
        back[k] = z
    out = final[0]
    for k in range(1, R):
        out = jnp.where(sub == k, final[k], out)
    return jnp.where(lane < at + R, out, 0.0), below, back, inside


def leaf(block, held):
    n = B // R
    w = [block[R * i:R * i + R, :] for i in range(n)]
    lane = lax.broadcasted_iota(jnp.int32, (R, B), 1)
    sub = lax.broadcasted_iota(jnp.int32, (R, B), 0)
    done = []
    for p in range(n):
        at = R * p
        last = p + 1 == n
        rows, below, back, inside = eliminate(w[p], w[p] if last else w[p + 1], held.at[p % 2], at, lane, sub)
        done.append(rows)
        if not last:
            w[p + 1] = below
        for i in range(p + 2, n):
            new = jnp.where(inside, 0.0, w[i])
            for j in reversed(range(R)):
                new = new - jnp.broadcast_to(w[i][:, at + j:at + j + 1], (R, B)) * back[j]
            w[i] = new
    return jnp.concatenate(done, axis=0)


def unit(n):
    return lax.broadcasted_iota(jnp.int32, (n, n), 0) == lax.broadcasted_iota(jnp.int32, (n, n), 1)


def halves():
    lower = [(i, j) for i in range(K // B) for j in range(i + 1)]
    return lower[:5], lower[5:]


def gram_step(place, parts_ref, sum_ref, packed_ref):
    total = (parts_ref[0] + parts_ref[1]) + (parts_ref[2] + parts_ref[3])
    sum_ref[...] = total
    for half, blocks in enumerate(halves()):
        slot = jnp.where(place[0] == half, 1, 0)
        for at, (i, j) in enumerate(blocks):
            packed_ref[slot, at] = dot(total[:, B * i:B * i + B], total[:, B * j:B * j + B], 0, 0)


def chol_inverse(place, own_ref, came_ref, *refs):
    loads, store = [], None
    if len(refs) > 3:
        many_ref, few_ref, out_ref, rows_ref, work, held, rows_held, in_sem, out_sem = refs
        loads = [pltpu.make_async_copy(many_ref.at[:, q], rows_held.at[q, :, :, pl.ds(FEW, K - FEW)], in_sem.at[q])
                 for q in range(4)]
        loads.append(pltpu.make_async_copy(few_ref, rows_held.at[:, :, :, pl.ds(0, FEW)], in_sem.at[4]))
        store = pltpu.make_async_copy(rows_held, rows_ref, out_sem)
    else:
        out_ref, work, held = refs
    for load in loads:
        load.start()
    for half, blocks in enumerate(halves()):
        for at, (i, j) in enumerate(blocks):
            entry = jnp.where(place[0] == half, own_ref[at], came_ref[at])
            work[B * i:B * i + B, B * j:B * j + B] = entry
            if i != j:
                work[B * j:B * j + B, B * i:B * i + B] = entry.T
    gram = work[...]
    diagonal = jnp.where(unit(K), gram, 0.0)
    along = lax.rsqrt(jnp.sum(diagonal, axis=0, keepdims=True))
    work[...] = gram * along * lax.rsqrt(jnp.sum(diagonal, axis=1, keepdims=True))

    def block(b, _):
        at = pl.multiple_of(b * B, B)
        if store is not None:
            @pl.when(b == 2)
            def _():
                for load in loads:
                    load.wait()
                store.start()
        low = leaf(work[pl.ds(at, B), pl.ds(at, B)], held)
        work[pl.ds(at, B), pl.ds(at, B)] = jnp.where(unit(B), 1.0, 0.0)
        top = dot(low, work[pl.ds(at, B), :], 1, 0)
        lane = lax.broadcasted_iota(jnp.int32, (B, K), 1)
        out_ref[pl.ds(at, B), :] = jnp.where(lane < at + B, top, 0.0) * along
        for last in range(K // B - 1):
            @pl.when(b == last)
            def _():
                to = B * (last + 1)
                work[to:, B * last:to] = jnp.zeros((K - to, B), jnp.float32)
                work[to:, :] = work[to:, :] - dot(top[:, to:], top, 0, 0)
        return 0

    lax.fori_loop(0, K // B, block, 0)
    if store is not None:
        store.wait()


VMEM = pl.BlockSpec(memory_space=pltpu.VMEM)
SMEM = pl.BlockSpec(memory_space=pltpu.SMEM)
HBM = pl.BlockSpec(memory_space=pl.ANY)


def core_place():
    return lax.axis_index("core").astype(jnp.int32).reshape(1)


def summed_gram(place, parts):
    return pl.pallas_call(
        gram_step,
        out_shape=[
            jax.ShapeDtypeStruct((ROWS, K), jnp.float32),
            jax.ShapeDtypeStruct((2, 5, B, B), jnp.float32),
        ],
        in_specs=[SMEM, VMEM],
        out_specs=[VMEM, VMEM],
        compiler_params=pltpu.CompilerParams(vmem_limit_bytes=12 * 1024 * 1024),
        cost_estimate=pl.CostEstimate(flops=2 * ROWS * K * K, bytes_accessed=8 * K * K, transcendentals=0),
    )(place, parts)


def inverse_factor(place, own, came, *rows):
    whole = jax.ShapeDtypeStruct((4, 8, ROWS, K), jnp.bfloat16)
    return pl.pallas_call(
        chol_inverse,
        out_shape=[jax.ShapeDtypeStruct((K, K), jnp.float32)] + ([whole] if rows else []),
        in_specs=[SMEM, VMEM, VMEM] + [HBM] * len(rows),
        out_specs=[VMEM] + ([HBM] if rows else []),
        scratch_shapes=[pltpu.VMEM((K, K), jnp.float32), pltpu.VMEM((2, R, R, B), jnp.float32)] + ([
            pltpu.VMEM(whole.shape, whole.dtype), pltpu.SemaphoreType.DMA((5,)), pltpu.SemaphoreType.DMA,
        ] if rows else []),
        compiler_params=pltpu.CompilerParams(vmem_limit_bytes=16 * 1024 * 1024),
        cost_estimate=pl.CostEstimate(flops=150 * K ** 3, bytes_accessed=8 * K * K, transcendentals=0),
    )(place, own, came, *rows)


def permute(values, where):
    places = [(z, y, x, c) for z in range(8) for y in range(4) for x in range(4) for c in range(2)]
    index = {place: i for i, place in enumerate(places)}
    return lax.ppermute(values, AXES, [(index[p], index[where(*p)]) for p in places])


def other_core(z, y, x, c):
    return z, y, x, 1 - c


def exchange(pieces, axes):
    return lax.all_to_all(pieces, axes, 0, 0, tiled=True)


def copies(values, axes):
    return jnp.broadcast_to(values[None], (lax.axis_size(axes),) + values.shape)


def up(z, y, x, c):
    return z, (y + 1) % 4, x, c


def down(z, y, x, c):
    return z, (y - 1) % 4, x, c


def gather_y(own):
    half = own.shape[0] // 2
    before, after = permute(own, up), permute(own, down)
    far = jnp.concatenate([permute(before[:half], up), permute(after[half:], down)], axis=0)
    return [own, after, far, before]


def small_pieces(own):
    far = permute(own, lambda z, y, x, c: (z, (y + 2) % 4, x, c))
    return [own, permute(own, down), far, permute(own, up)]


def in_order(pieces):
    rows, width = pieces[0].shape
    out = jnp.zeros((4 * rows, width), pieces[0].dtype)
    for step, piece in enumerate(pieces):
        out = lax.dynamic_update_slice_in_dim(out, piece, lax.rem(lax.axis_index("y") + step, 4) * rows, 0)
    return out


def column_place(z, y, x, c):
    return 2 * x + c, y, z // 2, z % 2


def gathered_rows(own):
    many, few = lax.optimization_barrier((in_order(small_pieces(own[:, FEW:])), own[:, :FEW]))
    many = lax.all_gather(many, "z", axis=0, tiled=True).reshape(8, 4, ROWS, K - FEW)
    return many, gather_y(exchange(copies(few, "z"), "z"))


def few_step(place, a_ref, *refs):
    pieces, out_ref, rows_ref = refs[:4], refs[4], refs[5]
    step = pl.program_id(1)

    @pl.when((pl.program_id(0) == 0) & (step == 0))
    def _():
        for j in range(4):
            rows_ref[lax.rem(place[0] + j, 4)] = pieces[j][...]

    a = a_ref[...].reshape(4 * ROWS, 8 * ROWS)
    b = rows_ref[step].reshape(8 * ROWS, FEW)
    term = jnp.dot(a, b, preferred_element_type=jnp.float32).reshape(out_ref.shape)

    @pl.when(step == 0)
    def _():
        out_ref[...] = term

    @pl.when(step > 0)
    def _():
        out_ref[...] += term


def product_few(factor, pieces):
    place = jnp.stack([lax.axis_index("y"), lax.axis_index("core")]).astype(jnp.int32)
    return pl.pallas_call(
        few_step,
        out_shape=[
            jax.ShapeDtypeStruct((2, 4, ROWS, FEW), jnp.float32),
            jax.ShapeDtypeStruct((4, 8, ROWS, FEW), jnp.bfloat16),
        ],
        grid_spec=pltpu.PrefetchScalarGridSpec(
            num_scalar_prefetch=1,
            grid=(2, 4),
            in_specs=[
                pl.BlockSpec((4, None, ROWS, 8 * ROWS), lambda h, q, place: (0, lax.rem(place[1] + 1 + h, 2), 0, q)),
            ] + [pl.BlockSpec((8, ROWS, FEW), lambda h, q, place: (0, 0, 0))] * 4,
            out_specs=[
                pl.BlockSpec((None, 4, ROWS, FEW), lambda h, q, place: (h, 0, 0, 0)),
                pl.BlockSpec((4, 8, ROWS, FEW), lambda h, q, place: (0, 0, 0, 0)),
            ],
        ),
        compiler_params=pltpu.CompilerParams(vmem_limit_bytes=16 * 1024 * 1024),
        cost_estimate=pl.CostEstimate(flops=2 * 8 * ROWS * M // 8 * FEW, bytes_accessed=8 * 1024 * 1024, transcendentals=0),
    )(place, factor.reshape(4, 2, ROWS, 32 * ROWS), *pieces)


def many_step(place, a_ref, b_ref, theirs_ref, mine_ref, a_held, b_held, total, a_sem, b_sem):
    steps, deep = 4, 8 * ROWS
    inward = [
        (
            pltpu.make_async_copy(a_ref.at[:, pl.ds(q * deep, deep)], a_held.at[q], a_sem.at[q]),
            pltpu.make_async_copy(b_ref.at[:, q], b_held.at[q], b_sem.at[q]),
        )
        for q in range(steps)
    ]
    for q in range(steps):
        for copy in inward[q]:
            copy.start()
    for q in range(steps):
        for copy in inward[q]:
            copy.wait()
        b = b_held[q].reshape(deep, K - FEW)
        term = jnp.dot(a_held[q], b, preferred_element_type=jnp.float32).reshape(total.shape)
        if q == 0:
            total[...] = term
        else:
            total[...] += term
    theirs_ref[...] = total[:, 1 - place[0]]
    mine_ref[...] = total[:, place[0]]


def product_many(factor, many, place):
    steps = 4
    part = jax.ShapeDtypeStruct((4, ROWS, K - FEW), jnp.float32)
    return pl.pallas_call(
        many_step,
        out_shape=[part, part],
        in_specs=[SMEM, HBM, HBM],
        out_specs=[VMEM, VMEM],
        scratch_shapes=[
            pltpu.VMEM((steps, 8 * ROWS, 8 * ROWS), jnp.bfloat16),
            pltpu.VMEM((steps, 8, ROWS, K - FEW), jnp.bfloat16),
            pltpu.VMEM((4, 2, ROWS, K - FEW), jnp.float32),
            pltpu.SemaphoreType.DMA((steps,)),
            pltpu.SemaphoreType.DMA((steps,)),
        ],
        compiler_params=pltpu.CompilerParams(vmem_limit_bytes=60 * 1024 * 1024),
        cost_estimate=pl.CostEstimate(flops=2 * 8 * ROWS * M // 8 * (K - FEW), bytes_accessed=12 * 1024 * 1024, transcendentals=0),
    )(place, factor, many)


def summed_product(factor, own):
    place = core_place()
    many, pieces = gathered_rows(own)
    both, ordered = product_few(factor, pieces)
    few = both[1] + permute(both[0], other_core)
    many, few = lax.optimization_barrier((many, few))
    theirs, mine = product_many(factor, many, place)
    total = jnp.concatenate([few, mine + permute(theirs, other_core)], axis=2)
    return summed_gram(place, exchange(total, "x")), (many, ordered)


def gram_inverse(packed, *rows):
    share = packed[1] + permute(packed[0], other_core)
    share = jnp.sum(exchange(share.reshape(16, 5 * B // 16, B), ("y", "x")), axis=0)
    share = jnp.sum(exchange(copies(share, "z"), "z"), axis=0)
    share = exchange(copies(share, ("y", "x")), ("y", "x")).reshape(5, B, B)
    return inverse_factor(core_place(), share, permute(share, other_core), *rows)


def shards(factor, basis):
    scale = math.sqrt(M)
    rows = lax.dynamic_slice_in_dim(basis, lax.axis_index(("x", "core")) * ROWS, ROWS, 0)
    (first, packed), _ = summed_product(factor, permute(rows, column_place))
    (inverse,), moved = lax.optimization_barrier((gram_inverse(packed), permute(first, column_place)))
    middle = (dot(moved, inverse, 1, 1) * scale).astype(jnp.bfloat16)
    (second, packed), gathered = summed_product(factor, middle)
    inverse, column_basis = gram_inverse(packed, *gathered)
    return dot(second, inverse, 1, 1) * scale, column_basis.reshape(32 * ROWS, K)


def solution(mesh):
    fine = jax.sharding.Mesh(mesh.devices.reshape(SIZES), AXES)
    return jax.shard_map(
        shards,
        mesh=fine,
        in_specs=(P(("z", "y"), ("x", "core")), P(("z", "y"), None)),
        out_specs=(P(AXES, None), P(("x", "core"), None)),
        check_vma=False,
    )
```

```python
import math

import jax
import jax.numpy as jnp
from jax import lax
from jax.experimental import pallas as pl
from jax.experimental.pallas import tpu as pltpu
from jax.sharding import PartitionSpec as P

M = 28672
K = 512
B = 128
R = 8
AXES = ("z", "y", "x", "core")
SIZES = (8, 4, 4, 2)
HALF = K // 2
FEW = 128
ROWS = M // 256


def dot(a, b, ca, cb):
    return lax.dot_general(a, b, (((ca,), (cb,)), ((), ())), precision=lax.Precision.HIGHEST,
                           preferred_element_type=jnp.float32)


def eliminate(top, below, held, at, lane, sub):
    wide = [jnp.broadcast_to(top[:, at + j:at + j + 1], (R, B)) for j in range(R)]
    for j in range(R):
        held[j] = wide[j]
    e = {(i, j): jnp.broadcast_to(held[j, i:i + 1, :], (R, B)) for i in range(R) for j in range(i + 1)}
    inside = (lane >= at) & (lane < at + R)
    rhs = jnp.where(inside, jnp.where(lane - at == sub, 1.0, 0.0), top)
    row = [jnp.broadcast_to(rhs[i:i + 1, :], (R, B)) for i in range(R)]
    ratio, solved, final = {}, [None] * R, [None] * R
    side = [jnp.broadcast_to(below[:, at + j:at + j + 1], (R, B)) for j in range(R)]
    below = jnp.where(inside, 0.0, below)
    for k in range(0, R, 2):
        a, b, c = e[k, k], e[k + 1, k], e[k + 1, k + 1]
        det = a * c - b * b
        over = 1.0 / det
        for i in range(k + 2, R):
            ratio[i, k] = (e[i, k] * c - e[i, k + 1] * b) * over
            ratio[i, k + 1] = (e[i, k + 1] * a - e[i, k] * b) * over
        for i in range(k + 2, R):
            for j in range(k + 2, i + 1):
                if i < k + 4:
                    one = (e[i, k] * c - e[i, k + 1] * b) * e[j, k]
                    two = (e[i, k + 1] * a - e[i, k] * b) * e[j, k + 1]
                    e[i, j] = e[i, j] - (one + two) * over
                else:
                    e[i, j] = e[i, j] - (ratio[i, k] * e[j, k] + ratio[i, k + 1] * e[j, k + 1])
            row[i] = row[i] - (ratio[i, k] * row[k] + ratio[i, k + 1] * row[k + 1])
        one = (side[k] * c - side[k + 1] * b) * over
        two = (side[k + 1] * a - side[k] * b) * over
        for j in range(k + 2, R):
            side[j] = side[j] - (one * e[j, k] + two * e[j, k + 1])
        below = below - (one * row[k] + two * row[k + 1])
        solved[k] = (c * row[k] - b * row[k + 1]) * over
        solved[k + 1] = (a * row[k + 1] - b * row[k]) * over
        root = lax.rsqrt(a)
        final[k] = row[k] * root
        final[k + 1] = (row[k + 1] - (b * root) * final[k]) * (lax.rsqrt(det) * (a * root))
    back = [None] * R
    for k in reversed(range(R)):
        z = solved[k]
        for i in reversed(range(k + 2 - k % 2, R)):
            z = z - ratio[i, k] * back[i]
        back[k] = z
    out = final[0]
    for k in range(1, R):
        out = jnp.where(sub == k, final[k], out)
    return jnp.where(lane < at + R, out, 0.0), below, back, inside


def leaf(block, held):
    n = B // R
    w = [block[R * i:R * i + R, :] for i in range(n)]
    lane = lax.broadcasted_iota(jnp.int32, (R, B), 1)
    sub = lax.broadcasted_iota(jnp.int32, (R, B), 0)
    done = []
    for p in range(n):
        at = R * p
        last = p + 1 == n
        rows, below, back, inside = eliminate(w[p], w[p] if last else w[p + 1], held.at[p % 2], at, lane, sub)
        done.append(rows)
        if not last:
            w[p + 1] = below
        for i in range(p + 2, n):
            new = jnp.where(inside, 0.0, w[i])
            for j in reversed(range(R)):
                new = new - jnp.broadcast_to(w[i][:, at + j:at + j + 1], (R, B)) * back[j]
            w[i] = new
    return jnp.concatenate(done, axis=0)


def unit(n):
    return lax.broadcasted_iota(jnp.int32, (n, n), 0) == lax.broadcasted_iota(jnp.int32, (n, n), 1)


def halves():
    lower = [(i, j) for i in range(K // B) for j in range(i + 1)]
    return lower[:5], lower[5:]


def gram_step(place, parts_ref, sum_ref, packed_ref):
    total = (parts_ref[0] + parts_ref[1]) + (parts_ref[2] + parts_ref[3])
    sum_ref[...] = total
    for half, blocks in enumerate(halves()):
        slot = jnp.where(place[0] == half, 1, 0)
        for at, (i, j) in enumerate(blocks):
            packed_ref[slot, at] = dot(total[:, B * i:B * i + B], total[:, B * j:B * j + B], 0, 0)


def chol_inverse(place, own_ref, came_ref, *refs):
    loads, store = [], None
    if len(refs) > 3:
        many_ref, few_ref, out_ref, rows_ref, work, held, rows_held, in_sem, out_sem = refs
        loads = [pltpu.make_async_copy(many_ref.at[:, q], rows_held.at[q, :, :, pl.ds(FEW, K - FEW)], in_sem.at[q])
                 for q in range(4)]
        loads.append(pltpu.make_async_copy(few_ref, rows_held.at[:, :, :, pl.ds(0, FEW)], in_sem.at[4]))
        store = pltpu.make_async_copy(rows_held, rows_ref, out_sem)
    else:
        out_ref, work, held = refs
    for load in loads:
        load.start()
    for half, blocks in enumerate(halves()):
        for at, (i, j) in enumerate(blocks):
            entry = jnp.where(place[0] == half, own_ref[at], came_ref[at])
            work[B * i:B * i + B, B * j:B * j + B] = entry
            if i != j:
                work[B * j:B * j + B, B * i:B * i + B] = entry.T
    gram = work[...]
    diagonal = jnp.where(unit(K), gram, 0.0)
    along = lax.rsqrt(jnp.sum(diagonal, axis=0, keepdims=True))
    work[...] = gram * along * lax.rsqrt(jnp.sum(diagonal, axis=1, keepdims=True))

    def block(b, _):
        at = pl.multiple_of(b * B, B)
        if store is not None:
            @pl.when(b == 2)
            def _():
                for load in loads:
                    load.wait()
                store.start()
        low = leaf(work[pl.ds(at, B), pl.ds(at, B)], held)
        work[pl.ds(at, B), pl.ds(at, B)] = jnp.where(unit(B), 1.0, 0.0)
        top = dot(low, work[pl.ds(at, B), :], 1, 0)
        lane = lax.broadcasted_iota(jnp.int32, (B, K), 1)
        out_ref[pl.ds(at, B), :] = jnp.where(lane < at + B, top, 0.0) * along
        for last in range(K // B - 1):
            @pl.when(b == last)
            def _():
                to = B * (last + 1)
                work[to:, B * last:to] = jnp.zeros((K - to, B), jnp.float32)
                work[to:, :] = work[to:, :] - dot(top[:, to:], top, 0, 0)
        return 0

    lax.fori_loop(0, K // B, block, 0)
    if store is not None:
        store.wait()


VMEM = pl.BlockSpec(memory_space=pltpu.VMEM)
SMEM = pl.BlockSpec(memory_space=pltpu.SMEM)
HBM = pl.BlockSpec(memory_space=pl.ANY)


def core_place():
    return lax.axis_index("core").astype(jnp.int32).reshape(1)


def summed_gram(place, parts):
    return pl.pallas_call(
        gram_step,
        out_shape=[
            jax.ShapeDtypeStruct((ROWS, K), jnp.float32),
            jax.ShapeDtypeStruct((2, 5, B, B), jnp.float32),
        ],
        in_specs=[SMEM, VMEM],
        out_specs=[VMEM, VMEM],
        compiler_params=pltpu.CompilerParams(vmem_limit_bytes=12 * 1024 * 1024),
        cost_estimate=pl.CostEstimate(flops=2 * ROWS * K * K, bytes_accessed=8 * K * K, transcendentals=0),
    )(place, parts)


def inverse_factor(place, own, came, *rows):
    whole = jax.ShapeDtypeStruct((4, 8, ROWS, K), jnp.bfloat16)
    return pl.pallas_call(
        chol_inverse,
        out_shape=[jax.ShapeDtypeStruct((K, K), jnp.float32)] + ([whole] if rows else []),
        in_specs=[SMEM, VMEM, VMEM] + [HBM] * len(rows),
        out_specs=[VMEM] + ([HBM] if rows else []),
        scratch_shapes=[pltpu.VMEM((K, K), jnp.float32), pltpu.VMEM((2, R, R, B), jnp.float32)] + ([
            pltpu.VMEM(whole.shape, whole.dtype), pltpu.SemaphoreType.DMA((5,)), pltpu.SemaphoreType.DMA,
        ] if rows else []),
        compiler_params=pltpu.CompilerParams(vmem_limit_bytes=(60 if rows else 16) * 1024 * 1024),
        cost_estimate=pl.CostEstimate(flops=150 * K ** 3, bytes_accessed=8 * K * K, transcendentals=0),
    )(place, own, came, *rows)


def permute(values, where):
    places = [(z, y, x, c) for z in range(8) for y in range(4) for x in range(4) for c in range(2)]
    index = {place: i for i, place in enumerate(places)}
    return lax.ppermute(values, AXES, [(index[p], index[where(*p)]) for p in places])


def other_core(z, y, x, c):
    return z, y, x, 1 - c


def exchange(pieces, axes):
    return lax.all_to_all(pieces, axes, 0, 0, tiled=True)


def copies(values, axes):
    return jnp.broadcast_to(values[None], (lax.axis_size(axes),) + values.shape)


def up(z, y, x, c):
    return z, (y + 1) % 4, x, c


def down(z, y, x, c):
    return z, (y - 1) % 4, x, c


def gather_y(own):
    half = own.shape[0] // 2
    before, after = permute(own, up), permute(own, down)
    far = jnp.concatenate([permute(before[:half], up), permute(after[half:], down)], axis=0)
    return [own, after, far, before]


def small_pieces(own):
    far = permute(own, lambda z, y, x, c: (z, (y + 2) % 4, x, c))
    return [own, permute(own, down), far, permute(own, up)]


def in_order(pieces):
    rows, width = pieces[0].shape
    out = jnp.zeros((4 * rows, width), pieces[0].dtype)
    for step, piece in enumerate(pieces):
        out = lax.dynamic_update_slice_in_dim(out, piece, lax.rem(lax.axis_index("y") + step, 4) * rows, 0)
    return out


def column_place(z, y, x, c):
    return 2 * x + c, y, z // 2, z % 2


def gathered_rows(own):
    many, few = lax.optimization_barrier((in_order(small_pieces(own[:, FEW:])), own[:, :FEW]))
    many = lax.all_gather(many, "z", axis=0, tiled=True).reshape(8, 4, ROWS, K - FEW)
    return many, gather_y(exchange(copies(few, "z"), "z"))


def few_step(place, a_ref, *refs):
    pieces, out_ref, rows_ref = refs[:4], refs[4], refs[5]
    step = pl.program_id(1)

    @pl.when((pl.program_id(0) == 0) & (step == 0))
    def _():
        for j in range(4):
            rows_ref[lax.rem(place[0] + j, 4)] = pieces[j][...]

    a = a_ref[...].reshape(4 * ROWS, 8 * ROWS)
    b = rows_ref[step].reshape(8 * ROWS, FEW)
    term = jnp.dot(a, b, preferred_element_type=jnp.float32).reshape(out_ref.shape)

    @pl.when(step == 0)
    def _():
        out_ref[...] = term

    @pl.when(step > 0)
    def _():
        out_ref[...] += term


def product_few(factor, pieces):
    place = jnp.stack([lax.axis_index("y"), lax.axis_index("core")]).astype(jnp.int32)
    return pl.pallas_call(
        few_step,
        out_shape=[
            jax.ShapeDtypeStruct((2, 4, ROWS, FEW), jnp.float32),
            jax.ShapeDtypeStruct((4, 8, ROWS, FEW), jnp.bfloat16),
        ],
        grid_spec=pltpu.PrefetchScalarGridSpec(
            num_scalar_prefetch=1,
            grid=(2, 4),
            in_specs=[
                pl.BlockSpec((4, None, ROWS, 8 * ROWS), lambda h, q, place: (0, lax.rem(place[1] + 1 + h, 2), 0, q)),
            ] + [pl.BlockSpec((8, ROWS, FEW), lambda h, q, place: (0, 0, 0))] * 4,
            out_specs=[
                pl.BlockSpec((None, 4, ROWS, FEW), lambda h, q, place: (h, 0, 0, 0)),
                pl.BlockSpec((4, 8, ROWS, FEW), lambda h, q, place: (0, 0, 0, 0)),
            ],
        ),
        compiler_params=pltpu.CompilerParams(vmem_limit_bytes=16 * 1024 * 1024),
        cost_estimate=pl.CostEstimate(flops=2 * 8 * ROWS * M // 8 * FEW, bytes_accessed=8 * 1024 * 1024, transcendentals=0),
    )(place, factor.reshape(4, 2, ROWS, 32 * ROWS), *pieces)


def many_step(place, a_ref, b_ref, theirs_ref, mine_ref, a_held, b_held, total, a_sem, b_sem):
    steps, deep = 4, 8 * ROWS
    inward = [
        (
            pltpu.make_async_copy(a_ref.at[:, pl.ds(q * deep, deep)], a_held.at[q], a_sem.at[q]),
            pltpu.make_async_copy(b_ref.at[:, q], b_held.at[q], b_sem.at[q]),
        )
        for q in range(steps)
    ]
    for q in range(steps):
        for copy in inward[q]:
            copy.start()
    for q in range(steps):
        for copy in inward[q]:
            copy.wait()
        b = b_held[q].reshape(deep, K - FEW)
        term = jnp.dot(a_held[q], b, preferred_element_type=jnp.float32).reshape(total.shape)
        if q == 0:
            total[...] = term
        else:
            total[...] += term
    theirs_ref[...] = total[:, 1 - place[0]]
    mine_ref[...] = total[:, place[0]]


def product_many(factor, many, place):
    steps = 4
    part = jax.ShapeDtypeStruct((4, ROWS, K - FEW), jnp.float32)
    return pl.pallas_call(
        many_step,
        out_shape=[part, part],
        in_specs=[SMEM, HBM, HBM],
        out_specs=[VMEM, VMEM],
        scratch_shapes=[
            pltpu.VMEM((steps, 8 * ROWS, 8 * ROWS), jnp.bfloat16),
            pltpu.VMEM((steps, 8, ROWS, K - FEW), jnp.bfloat16),
            pltpu.VMEM((4, 2, ROWS, K - FEW), jnp.float32),
            pltpu.SemaphoreType.DMA((steps,)),
            pltpu.SemaphoreType.DMA((steps,)),
        ],
        compiler_params=pltpu.CompilerParams(vmem_limit_bytes=60 * 1024 * 1024),
        cost_estimate=pl.CostEstimate(flops=2 * 8 * ROWS * M // 8 * (K - FEW), bytes_accessed=12 * 1024 * 1024, transcendentals=0),
    )(place, factor, many)


def summed_product(factor, own):
    place = core_place()
    many, pieces = gathered_rows(own)
    both, ordered = product_few(factor, pieces)
    few = both[1] + permute(both[0], other_core)
    many, few = lax.optimization_barrier((many, few))
    theirs, mine = product_many(factor, many, place)
    total = jnp.concatenate([few, mine + permute(theirs, other_core)], axis=2)
    return summed_gram(place, exchange(total, "x")), (many, ordered)


def gram_inverse(packed, *rows):
    share = packed[1] + permute(packed[0], other_core)
    share = jnp.sum(exchange(share.reshape(16, 5 * B // 16, B), ("y", "x")), axis=0)
    share = jnp.sum(exchange(copies(share, "z"), "z"), axis=0)
    share = exchange(copies(share, ("y", "x")), ("y", "x")).reshape(5, B, B)
    return inverse_factor(core_place(), share, permute(share, other_core), *rows)


def shards(factor, basis):
    scale = math.sqrt(M)
    rows = lax.dynamic_slice_in_dim(basis, lax.axis_index(("x", "core")) * ROWS, ROWS, 0)
    (first, packed), _ = summed_product(factor, permute(rows, column_place))
    (inverse,), moved = lax.optimization_barrier((gram_inverse(packed), permute(first, column_place)))
    middle = (dot(moved, inverse, 1, 1) * scale).astype(jnp.bfloat16)
    (second, packed), gathered = summed_product(factor, middle)
    inverse, column_basis = gram_inverse(packed, *gathered)
    return dot(second, inverse, 1, 1) * scale, column_basis.reshape(32 * ROWS, K)


def solution(mesh):
    fine = jax.sharding.Mesh(mesh.devices.reshape(SIZES), AXES)
    return jax.shard_map(
        shards,
        mesh=fine,
        in_specs=(P(("z", "y"), ("x", "core")), P(("z", "y"), None)),
        out_specs=(P(AXES, None), P(("x", "core"), None)),
        check_vma=False,
    )
```
